128 devices in a mesh: samp: 8 (over x, core), par: 16 (over y, z).
Axes of the slice: x: 4, y: 4, z: 4, core: 2. Of those that a mesh axis runs over, the one named last changes fastest.
Arguments:
- stream: float32 [512, 25, 512], P('samp'), may hold values from -48 to 48
- weight_in: bfloat16 [512, 2048], P('samp', 'par'), may hold values from -0.25 to 0.25
- weight_out: bfloat16 [2048, 512], P('par'), may hold values from -0.125 to 0.125
- readout: float32 [512], replicated, may hold values from -5 to 5
- spins: int32 [512, 100], replicated, may hold values from 0 to 1
- offdiag: float32 [512], replicated, may hold values from -18 to 18
Outputs:
- update: float32 [512, 2048], P('samp', 'par')
The draws below stay inside these ranges and needn't reach their ends.
Inputs may be any that keep to these rules, and one draw needn't show every extreme that they name: `spins`: 1 marks an up spin, 0 a down spin.
All inputs are finite; a program needn't handle non-finite values.
Results may differ from the reference program's by a relative error of at most 0.02.
The reference program's roundings to bfloat16 on the way count: a program that leaves them out, or rounds other values in their place, can miss the bound.
Values may be sent and summed in bfloat16 or wider, within the bound.
A program may use at most 384 MiB of HBM per device.

```python
import math
import jax
import jax.numpy as jnp
from jax import lax

D = 512
FF = 2048
LSIDE = 10
TOK = 25
SITES = 100
M = 512


mode_count = 16


def feature_scales(key, top_ratio):
    column_pos = jnp.arange(D, dtype=jnp.float32) / (D - 1)
    ramp_scale = jnp.exp(jnp.log(top_ratio) * column_pos)
    jitter = jax.random.uniform(key, (D,), jnp.float32, 0.7, 1.4)
    return ramp_scale * jitter


def combine_modes(base_field, loadings, modes, noise_field):
    values = base_field[None, :, :] + noise_field
    for index in range(mode_count):
        weight = 2.0 ** (-0.5 * (index + 1))
        values = values + (weight * loadings[:, index])[:, None, None] * modes[index][None, :, :]
    return values


def draw_stream(key, part):
    key = jax.random.fold_in(key, 11)
    base_key, mode_key, load_key, noise_key, scale_key = jax.random.split(key, 5)
    base_field = jnp.clip(jax.random.normal(base_key, (TOK, D), jnp.float32), -4.0, 4.0)
    modes = jnp.clip(jax.random.normal(mode_key, (mode_count, TOK, D), jnp.float32), -4.0, 4.0)
    loadings = jnp.clip(jax.random.normal(load_key, (M, mode_count), jnp.float32), -4.0, 4.0)
    noise_field = 0.3 * jnp.clip(jax.random.normal(noise_key, (M, TOK, D), jnp.float32), -4.0, 4.0)
    scales = feature_scales(scale_key, 8.0)
    values = combine_modes(base_field, loadings, modes, noise_field)
    return jnp.clip(values * scales, -48.0, 48.0)


def touch_ends(values, key, least, largest):
    extent = values.shape
    spot = [jax.random.randint(jax.random.fold_in(key, axis), (), 0, extent[axis]) for axis in range(len(extent))]
    values = values.at[tuple(spot)].set(least)
    longest = extent.index(max(extent))
    spot[longest] = (spot[longest] + 1) % extent[longest]
    return values.at[tuple(spot)].set(largest)


def level_of(rng, extent, shards, smallest, largest):
    def one(dim, parts):
        heights = jax.random.uniform(jax.random.fold_in(jax.random.fold_in(rng, 6), dim), (parts,), jnp.float32, smallest / len(shards), largest / len(shards))
        return jnp.repeat(jnp.exp(heights), extent[dim] // parts).reshape((-1,) + (1,) * (len(extent) - dim - 1))

    level = one(*shards[0])
    for cut in shards[1:]:
        level = level * one(*cut)
    return level


def bell_draw(key, shape, width, limit, cuts=(), kind=jnp.bfloat16):
    drawn = jax.random.normal(key, shape, jnp.float32) * width
    if len(cuts) > 0:
        drawn = level_of(key, shape, cuts, -0.22, 0.18) * drawn
    return jnp.clip(drawn, min=-limit, max=limit).astype(kind)


def setup_inputs(seed: int = 0) -> dict:
    arg_keys = jax.random.split(jax.random.key(seed), 7)
    stream = draw_stream(jax.random.fold_in(arg_keys[6], 71), 0)
    weight_in = bell_draw(arg_keys[1], (D, FF), D ** -0.5, 0.25, ((0, 8), (1, 16)))
    weight_out = bell_draw(arg_keys[2], (FF, D), FF ** -0.5, 0.125, ((0, 16),))
    readout = bell_draw(arg_keys[3], (D,), 1.0, 5.0, (), jnp.float32)
    spins = touch_ends(jax.random.randint(arg_keys[4], (M, SITES), 0, 2), jax.random.fold_in(arg_keys[4], 1), 0, 1).astype(jnp.int32)
    offdiag = bell_draw(arg_keys[5], (M,), 3.0, 18.0, (), jnp.float32)
    return dict(stream=stream, weight_in=weight_in, weight_out=weight_out, readout=readout, spins=spins, offdiag=offdiag)


EPSILON = 1e-05
SHIFT_RATIO = 0.1
SECOND_RATIO = 0.5

def norm_rows(values):
    row_mean = lax.optimization_barrier(jnp.mean(values, axis=-1, keepdims=True))
    centered = values - row_mean
    variance = lax.optimization_barrier(jnp.mean(centered * centered, axis=-1, keepdims=True))
    return centered * lax.rsqrt(variance + EPSILON)

def gelu_back(preact, cotangent):
    _, backward = jax.vjp(jax.nn.gelu, preact)
    return backward(cotangent)[0]

def local_energy(spins, offdiag):
    spin_signs = (2 * spins - 1).astype(jnp.float32).reshape(spins.shape[0], LSIDE, LSIDE)
    right_spin = jnp.roll(spin_signs, -1, axis=2)
    down_spin = jnp.roll(spin_signs, -1, axis=1)
    diag_one = jnp.roll(down_spin, -1, axis=2)
    diag_two = jnp.roll(down_spin, 1, axis=2)
    near_bonds = lax.optimization_barrier(jnp.sum(spin_signs * right_spin + spin_signs * down_spin, axis=(1, 2)))
    far_bonds = lax.optimization_barrier(jnp.sum(spin_signs * diag_one + spin_signs * diag_two, axis=(1, 2)))
    return 0.25 * (near_bonds + SECOND_RATIO * far_bonds) + offdiag

def reference(stream, weight_in, weight_out, readout, spins, offdiag):
    hidden = norm_rows(stream).astype(jnp.bfloat16).reshape(M * TOK, D)
    preact = jnp.dot(hidden.astype(jnp.float32), weight_in.astype(jnp.float32), preferred_element_type=jnp.float32)
    activated = jax.nn.gelu(preact).astype(jnp.bfloat16)
    summed = jnp.dot(activated.astype(jnp.float32), weight_out.astype(jnp.float32), preferred_element_type=jnp.float32)
    signal = (readout * jnp.tanh(summed)).astype(jnp.bfloat16)
    backward = lax.dot_general(signal.astype(jnp.float32), weight_out.astype(jnp.float32), (((1,), (1,)), ((), ())), preferred_element_type=jnp.float32)
    delta_rows = gelu_back(preact, backward).astype(jnp.bfloat16).reshape(M, TOK, FF)
    features = hidden.reshape(M, TOK, D).astype(jnp.float32)
    block_width = 128
    block_count = FF // block_width
    norm_scale = 1.0 / math.sqrt(M)

    def make_panel(block_index):
        delta_block = lax.dynamic_slice_in_dim(delta_rows, (block_index * block_width).astype(jnp.int32), block_width, 2).astype(jnp.float32)
        gradients = jnp.einsum('std,stf->sdf', features, delta_block)
        gradients = lax.optimization_barrier(gradients.astype(jnp.bfloat16)).astype(jnp.float32)
        sample_mean = lax.optimization_barrier(jnp.mean(gradients, axis=0, keepdims=True))
        return ((gradients - sample_mean) * norm_scale).astype(jnp.bfloat16).reshape(M, D * block_width)

    def add_gram(carry_sum, block_index):
        widened = make_panel(block_index).astype(jnp.float32)
        term = lax.dot_general(widened.astype(jnp.float32), widened.astype(jnp.float32), (((1,), (1,)), ((), ())), precision=lax.Precision.HIGHEST, preferred_element_type=jnp.float32)
        return (carry_sum + term, None)
    blocks = jnp.arange(block_count, dtype=jnp.int32)
    gram, _ = lax.scan(add_gram, jnp.zeros((M, M), jnp.float32), blocks)
    diag_shift = SHIFT_RATIO * jnp.trace(gram) / M
    system = gram + diag_shift * jnp.eye(M, dtype=jnp.float32)
    energies = local_energy(spins, offdiag)
    target = ((energies - jnp.mean(energies)) * norm_scale)[:, None]
    lower_factor = jnp.linalg.cholesky(system)
    forward_solved = lax.linalg.triangular_solve(lower_factor, target, left_side=True, lower=True)
    solution = lax.linalg.triangular_solve(lower_factor, forward_solved, left_side=True, lower=True, transpose_a=True)
    coeffs = solution[:, 0].astype(jnp.bfloat16)
    step_scale = -math.sqrt(D * FF)

    def block_update(carry_sum, block_index):
        centered = make_panel(block_index)
        result = jnp.dot(coeffs[None, :].astype(jnp.float32), centered.astype(jnp.float32), preferred_element_type=jnp.float32).reshape(D, block_width)
        return (carry_sum, result * step_scale)
    _, pieces = lax.scan(block_update, jnp.zeros((), jnp.float32), blocks)
    return jnp.moveaxis(pieces, 0, 1).reshape(D, FF)
```

```python
import functools
import math

import jax
import jax.numpy as jnp
from jax import lax
from jax.experimental import pallas as pl
from jax.experimental.pallas import tpu as pltpu
from jax.sharding import PartitionSpec as P

D = 512
FF = 2048
EPSILON = 1e-05
SHIFT_RATIO = 0.1
SECOND_RATIO = 0.5
MESH = pl.DeviceIdType.MESH
F32 = jnp.float32
BF16 = jnp.bfloat16
HI = lax.Precision.HIGHEST


def dot_nn(a, b):
    return lax.dot_general(a, b, (((1,), (0,)), ((), ())), precision=HI, preferred_element_type=F32)


def dot_nt(a, b):
    return lax.dot_general(a, b, (((1,), (1,)), ((), ())), precision=HI, preferred_element_type=F32)


def thirds(values):
    high = values.astype(BF16).astype(F32)
    rest = values - high
    middle = rest.astype(BF16).astype(F32)
    return high, middle, rest - middle


def outer(left, right):
    a, b, c = thirds(left)
    d, e, f = thirds(right)
    lhs = jnp.concatenate([a, a, b, a, b, c], axis=0).astype(BF16)
    rhs = jnp.concatenate([d, e, d, f, e, d], axis=0).astype(BF16)
    return lax.dot_general(lhs, rhs, (((0,), (0,)), ((), ())), preferred_element_type=F32)


def spread_column(values, at):
    return jnp.broadcast_to(values[:, at : at + 1], (8, 128))


def sweep_block(block):
    lane = lax.broadcasted_iota(jnp.int32, (8, 128), 1)
    sub = lax.broadcasted_iota(jnp.int32, (8, 128), 0)
    rows = [block[8 * r : 8 * r + 8, :] for r in range(16)]
    for g in range(16):
        panel = rows[g]
        before = panel
        splat = [spread_column(panel, 8 * g + m) for m in range(8)]
        for i in range(8):
            unit = jnp.where(sub == i, 1.0, 0.0)
            pivot = jnp.broadcast_to(splat[i][i : i + 1, :], (8, 128))
            factor = (splat[i] - unit) * (1.0 / pivot)
            panel = jnp.where(lane == 8 * g + i, unit, panel)
            panel = panel - factor * jnp.broadcast_to(panel[i : i + 1, :], (8, 128))
            for m in range(i + 1, 8):
                splat[m] = splat[m] - factor * jnp.broadcast_to(splat[m][i : i + 1, :], (8, 128))
        inside = (lane >= 8 * g) & (lane < 8 * g + 8)
        panel = jnp.where(inside, -panel, panel)
        change = outer(before, panel)
        for r in range(16):
            if r == g:
                continue
            kept = jnp.where(inside, 0.0, rows[r])
            if r == g + 1:
                for m in range(8):
                    kept = kept - spread_column(rows[r], 8 * g + m) * jnp.broadcast_to(panel[m : m + 1, :], (8, 128))
                rows[r] = kept
            else:
                rows[r] = kept - change[8 * r : 8 * r + 8, :]
        rows[g] = panel
    return jnp.concatenate(rows, axis=0)


def solve_kernel(shift_ratio, scale, samples, gram_ref, target_ref, cent_hbm, out_ref, a_ref, w_ref, cent, sems):
    blocks = samples // 128
    chunks = sems.shape[0]
    wide = cent.shape[1] // chunks

    def load(m):
        at = pl.ds(m * wide, wide)
        return pltpu.make_async_copy(cent_hbm.at[:, at], cent.at[:, at], sems.at[m])

    for m in range(chunks):
        load(m).start()
    eye = lax.broadcasted_iota(jnp.int32, (128, 128), 0) == lax.broadcasted_iota(jnp.int32, (128, 128), 1)
    base = [0]
    for k in range(blocks):
        base.append(base[-1] + samples - 128 * k)
    trace = jnp.zeros((1, 1), F32)
    for k in range(blocks):
        trace += jnp.sum(jnp.where(eye, gram_ref[base[k] : base[k] + 128, :], 0.0), axis=(0, 1), keepdims=True)
    shift = shift_ratio * trace / samples
    shift = jnp.where(eye, jnp.broadcast_to(shift, (128, 128)), 0.0)
    rhs = []
    for k in range(blocks):
        a_ref[base[k] : base[k] + 128, :] = gram_ref[base[k] : base[k] + 128, :] + shift
        if k < blocks - 1:
            a_ref[base[k] + 128 : base[k + 1], :] = gram_ref[base[k] + 128 : base[k + 1], :]
        rhs.append(jnp.broadcast_to(target_ref[0:1, 128 * k : 128 * k + 128], (8, 128)))
    for k in range(blocks):
        inv = -sweep_block(a_ref[base[k] : base[k] + 128, :])
        if k < blocks - 1:
            below = a_ref[base[k] + 128 : base[k + 1], :]
            w = dot_nn(below, inv)
            w_ref[base[k] + 128 : base[k + 1], :] = w
            drop = dot_nt(rhs[k], w)
            for j in range(k + 1, blocks):
                at = 128 * (j - k - 1)
                a_ref[base[j] : base[j + 1], :] -= dot_nt(w[at:], below[at : at + 128])
                rhs[j] = rhs[j] - drop[:, at : at + 128]
        rhs[k] = dot_nn(rhs[k], inv)
    found = [None] * blocks
    for k in reversed(range(blocks)):
        x = rhs[k]
        for i in range(k + 1, blocks):
            r = base[k] + 128 * (i - k)
            x = x - dot_nn(found[i], w_ref[r : r + 128, :])
        found[k] = x
    coeffs = jnp.concatenate(found, axis=1).astype(BF16)
    for m in range(chunks):
        load(m).wait()
        part = jnp.dot(coeffs, cent[:, m * wide : (m + 1) * wide], preferred_element_type=F32) * scale
        for i in range(wide // 128):
            r = m * wide // 128 + i
            out_ref[r : r + 1, :] = part[0:1, 128 * i : 128 * (i + 1)]


def solve(gram, target, centered):
    samples, width = centered.shape
    blocks = samples // 128
    rows = blocks * (blocks + 1) // 2 * 128
    vmem = pl.BlockSpec(memory_space=pltpu.VMEM)
    return pl.pallas_call(
        functools.partial(solve_kernel, SHIFT_RATIO, -math.sqrt(D * FF), samples),
        out_shape=jax.ShapeDtypeStruct((width // 128, 128), F32),
        in_specs=[vmem, vmem, pl.BlockSpec(memory_space=pl.ANY)],
        out_specs=vmem,
        scratch_shapes=[
            pltpu.VMEM((rows, 128), F32),
            pltpu.VMEM((rows, 128), F32),
            pltpu.VMEM((samples, width), BF16),
            pltpu.SemaphoreType.DMA((8,)),
        ],
        compiler_params=pltpu.CompilerParams(vmem_limit_bytes=60 << 20),
        name="solve",
    )(gram, target, centered)


GROUP = 4
WIDE = 8 * 65


def enter(ids):
    barrier = pltpu.get_barrier_semaphore()
    for device in ids:
        pl.semaphore_signal(barrier, inc=1, device_id=device, device_id_type=MESH)
    pl.semaphore_wait(barrier, len(ids))


def remote(src, dst, send, recv, device):
    copy = pltpu.make_async_remote_copy(
        src_ref=src, dst_ref=dst, send_sem=send, recv_sem=recv, device_id=device, device_id_type=MESH
    )
    copy.start()
    return copy


def describe(src, dst, send, recv, device):
    return pltpu.make_async_remote_copy(
        src_ref=src, dst_ref=dst, send_sem=send, recv_sem=recv, device_id=device, device_id_type=MESH
    )


def each(first, last, body):
    def step(k, carry):
        body(k)
        return carry

    lax.fori_loop(first, last, step, 0)


def forward_kernel(
    stream_ref, win_ref, wout_ref, readout_ref, hall_ref, dl_ref,
    win, wout, hid, ht, slope, acc, dsend,
    xs, xr, ws, wr, vs, vr, wws, wwr, vvs, vvr, sws, swr, svs, svr, hs, hr, ls, lr, own,
):
    s, p = lax.axis_index("samp"), lax.axis_index("par")
    x, c = s // 2, lax.rem(s, 2)
    y, z = p // 4, lax.rem(p, 4)
    sibling = s + 1 - 2 * c
    n = 16
    groups, tokens = 16, 25
    rows = hid.shape[0]
    enter([(s, lax.rem(p + k, n)) for k in range(1, n)] + [(lax.rem(s + k, 8), p) for k in range(1, 8)])

    def at(a, b):
        return lax.rem(y + a, 4) * 4 + lax.rem(z + b, 4)

    def origin(a, b):
        return at(4 - a, 4 - b)

    def xcopy(k):
        return describe(win_ref, win.at[p, x, c], xs.at[k - 1], xr.at[k - 1], (lax.rem(s + 2 * k, 8), p))

    def w_first(k):
        return describe(win.at[p, :, c], win.at[p, :, c], ws.at[k - 1], wr.at[k - 1], (s, at(k, 0)))

    def w_then(a, m):
        q, i = origin(a, 0), 3 * a + m - 1
        return describe(win.at[q, :, c], win.at[q, :, c], wws.at[i], wwr.at[i], (s, at(0, m)))

    def v_first(k):
        return describe(wout.at[p, c], wout.at[p, c], vs.at[k - 1], vr.at[k - 1], (s, at(0, k)))

    def v_then(b, m):
        q, i = origin(0, b), 3 * b + m - 1
        return describe(wout.at[q, c], wout.at[q, c], vvs.at[i], vvr.at[i], (s, at(m, 0)))

    def w_across(i):
        q = origin(i // 4, lax.rem(i, 4))
        return describe(win.at[q, :, c], win.at[q, :, c], sws.at[i], swr.at[i], (sibling, p))

    def v_across(i):
        q = origin(i // 4, lax.rem(i, 4))
        return describe(wout.at[q, c], wout.at[q, c], svs.at[i], svr.at[i], (sibling, p))

    def hcopy(k):
        to = lax.rem(s + k, 8)
        return describe(ht.at[to], hall_ref.at[s], hs.at[k - 1], hr.at[k - 1], (to, p))

    def lcopy(k):
        q = lax.rem(p + k, n)
        return describe(dsend.at[q], dl_ref.at[p], ls.at[k - 1], lr.at[k - 1], (s, q))

    mine_w = pltpu.make_async_copy(win_ref, win.at[p, x, c], own.at[0])
    mine_v = pltpu.make_async_copy(wout_ref.at[pl.ds(pl.multiple_of(64 * c, 64), 64)], wout.at[p, c], own.at[1])
    mine_w.start()
    mine_v.start()
    each(1, 4, lambda k: xcopy(k).start())
    mine_v.wait()
    each(1, 4, lambda k: v_first(k).start())
    each(1, 4, lambda m: v_then(0, m).start())
    v_across(0).start()
    mine_w.wait()

    def prepare(pair):
        values = stream_ref[:, pl.ds(pl.multiple_of(8 * pair, 8), 8), :]
        mean = jnp.mean(values, axis=-1, keepdims=True)
        centered = values - mean
        variance = jnp.mean(centered * centered, axis=-1, keepdims=True)
        scaled = centered * lax.rsqrt(variance + EPSILON)
        for half in range(2):
            g = 2 * pair + half
            hidden = jnp.concatenate(
                [scaled[t, 4 * half : 4 * half + 4] for t in range(tokens)] + [jnp.zeros((128 - 4 * tokens, 512), F32)], axis=0
            )

            @pl.when(g == p)
            def _():
                hid[...] = hidden[:rows].astype(BF16)

            flipped = jnp.transpose(hidden).astype(BF16)
            for q in range(8):
                ht[q, g] = flipped[64 * q : 64 * (q + 1), :]

    def open_w():
        each(1, 4, lambda k: xcopy(k).wait_recv())
        each(1, 4, lambda k: w_first(k).start())
        each(1, 4, lambda m: w_then(0, m).start())
        w_across(0).start()

    def pass_v(k):
        v_first(k).wait_recv()
        each(1, 4, lambda m: v_then(k, m).start())
        v_across(k).start()

    def pass_w(k):
        w_first(k).wait_recv()
        each(1, 4, lambda m: w_then(k, m).start())
        w_across(4 * k).start()

    def work(step):
        prepare(step)

        @pl.when(step == 0)
        def _():
            open_w()

        @pl.when(step == 2)
        def _():
            each(1, 4, pass_v)

        @pl.when(step == 4)
        def _():
            each(1, 4, pass_w)

    each(0, groups // 2, work)
    each(1, 8, lambda k: hcopy(k).start())
    mine_h = pltpu.make_async_copy(ht.at[s], hall_ref.at[s], own.at[2])
    mine_h.start()
    acc[...] = jnp.zeros_like(acc)

    def take(i):
        a, b = i // 4, lax.rem(i, 4)

        @pl.when(b > 0)
        def _():
            w_then(a, b).wait_recv()
            w_across(i).start()

        @pl.when(a > 0)
        def _():
            v_then(b, a).wait_recv()
            v_across(i).start()

    def compute(i):
        q = origin(i // 4, lax.rem(i, 4))
        w_across(i).wait_recv()
        v_across(i).wait_recv()
        preact = jnp.dot(hid[...], win[q].reshape(512, 128), preferred_element_type=F32)
        active, pull = jax.vjp(jax.nn.gelu, preact)
        slope[q] = pull(jnp.ones_like(preact))[0]
        acc[...] += jnp.dot(active.astype(BF16), wout[q].reshape(128, 512), preferred_element_type=F32)

    take(0)

    def both(i):
        take(i)
        compute(i - 1)

    each(1, n, both)
    compute(n - 1)
    signal = (readout_ref[...] * jnp.tanh(acc[...])).astype(BF16)

    def back(k):
        j = lax.rem(p // 2 + k, 8)
        weights = wout[pl.ds(2 * j, 2)].reshape(256, 512)
        backward = lax.dot_general(signal, weights, (((1,), (1,)), ((), ())), preferred_element_type=F32)
        for u in range(2):
            q = 2 * j + u
            dsend[q] = (backward[:, 128 * u : 128 * (u + 1)] * slope[q]).astype(BF16)

            @pl.when(q != p)
            def _():
                lcopy(lax.rem(q - p + n, n)).start()

    each(1, 9, back)
    dl_ref[p] = dsend[p]
    each(1, n, lambda k: lcopy(k).wait())
    each(1, 8, lambda k: hcopy(k).wait())
    mine_h.wait()
    each(1, 4, lambda k: xcopy(k).wait_send())
    each(1, 4, lambda k: w_first(k).wait_send())
    each(1, 4, lambda k: v_first(k).wait_send())
    each(0, 4, lambda k: each(1, 4, lambda m: w_then(k, m).wait_send()))
    each(0, 4, lambda k: each(1, 4, lambda m: v_then(k, m).wait_send()))
    each(0, n, lambda i: w_across(i).wait_send())
    each(0, n, lambda i: v_across(i).wait_send())


def forward(stream, weight_in, weight_out, readout):
    rows = 112
    sem = pltpu.SemaphoreType.DMA
    vmem = pl.BlockSpec(memory_space=pltpu.VMEM)
    return pl.pallas_call(
        forward_kernel,
        out_shape=[jax.ShapeDtypeStruct((8, 16, 64, 128), BF16), jax.ShapeDtypeStruct((16, rows, 128), BF16)],
        in_specs=[vmem] * 4,
        out_specs=[pl.BlockSpec(memory_space=pl.ANY), vmem],
        scratch_shapes=[
            pltpu.VMEM((16, 4, 2, 64, 128), BF16),
            pltpu.VMEM((16, 2, 64, 512), BF16),
            pltpu.VMEM((rows, 512), BF16),
            pltpu.VMEM((8, 16, 64, 128), BF16),
            pltpu.VMEM((16, rows, 128), F32),
            pltpu.VMEM((rows, 512), F32),
            pltpu.VMEM((16, rows, 128), BF16),
        ]
        + [sem((3,))] * 6
        + [sem((12,))] * 4
        + [sem((16,))] * 4
        + [sem((7,))] * 2
        + [sem((15,))] * 2
        + [sem((3,))],
        compiler_params=pltpu.CompilerParams(collective_id=3, has_side_effects=True, vmem_limit_bytes=56 << 20),
        name="forward",
    )(stream, weight_in, weight_out, readout)


def gather_gram_kernel(
    hall_ref, dl_ref, cent_out, gram_ref, ht, dall, grad, cent, part_ref, twin, first, second,
    sr, rr, sl, rl, fr, qr, fl, ql, bs, br, s0, r0, s1, r1, s2, r2, s3, r3, s4, r4, own, outs,
):
    s, p = lax.axis_index("samp"), lax.axis_index("par")
    sibling = s + 1 - 2 * lax.rem(s, 2)
    right, left, far = lax.rem(s + 2, 8), lax.rem(s + 6, 8), lax.rem(s + 4, 8)
    pars = [lax.rem(p + k, 16) for k in range(1, 16)]
    samps = [lax.rem(s + k, 8) for k in range(1, 8)]
    dims, width, rows, tokens, samples = 64, 128, 112, 25, 512
    norm_scale = 1.0 / math.sqrt(samples)
    mine_h = pltpu.make_async_copy(hall_ref, ht, own.at[0])
    mine_d = pltpu.make_async_copy(dl_ref, dall.at[s], own.at[1])
    mine_h.start()
    mine_d.start()
    enter([(s, q) for q in pars] + [(q, p) for q in samps])

    def part(origin, c):
        return dall.at[origin, pl.ds(pl.multiple_of(4 * c, 4), 4)]

    def to_right(c):
        return describe(part(s, c), part(s, c), sr.at[c], rr.at[c], (right, p))

    def to_left(c):
        return describe(part(s, c), part(s, c), sl.at[c], rl.at[c], (left, p))

    def on_right(c):
        return describe(part(left, c), part(left, c), fr.at[c], qr.at[c], (right, p))

    def on_left(c):
        return describe(part(right, c + 2), part(right, c + 2), fl.at[c], ql.at[c], (left, p))

    def across(origin, c, slot):
        return describe(part(origin, c), part(origin, c), bs.at[slot], br.at[slot], (sibling, p))

    mine_d.wait()

    def begin(c):
        to_right(c).start()
        to_left(lax.rem(c + 2, 4)).start()

    each(0, 4, begin)
    each(0, 4, lambda c: across(s, c, c).start())
    mine_h.wait()

    lane = lax.broadcasted_iota(jnp.int32, (dims, width), 1)
    keep = [(lax.rem(lane, GROUP) == i) & (lane < tokens * GROUP) for i in range(GROUP)]
    fill = jnp.zeros((width - rows, 128), BF16)
    nothing = jnp.zeros((dims, width), BF16)

    def make(origin, c):
        for u in range(4):
            group = 4 * c + u
            flipped = ht[origin, group]
            delta = jnp.concatenate([dall[origin, group], fill], axis=0)
            stack = jnp.concatenate([jnp.where(keep[i], flipped, nothing) for i in range(GROUP)], axis=0)
            grads = jnp.dot(stack, delta, preferred_element_type=F32).astype(BF16).astype(F32)
            for i in range(GROUP):
                grad[pl.ds(64 * origin + GROUP * group + i, dims, stride=WIDE), :] = grads[dims * i : dims * (i + 1), :]

    each(0, 4, lambda c: make(s, c))

    def near(c):
        d = lax.rem(c + 2, 4)
        to_right(c).wait_recv()

        @pl.when(c < 2)
        def _():
            on_right(c).start()

        across(left, c, 4 + c).start()
        to_left(d).wait_recv()

        @pl.when(c < 2)
        def _():
            on_left(c).start()

        across(right, d, 8 + d).start()
        make(left, c)
        make(right, d)

    each(0, 4, near)

    def beside(c):
        across(s, c, c).wait_recv()
        make(sibling, c)

    each(0, 4, beside)

    def opposite(c):
        on_right(c).wait_recv()
        across(far, c, 12 + c).start()
        on_left(c).wait_recv()
        across(far, c + 2, 14 + c).start()
        make(far, c)
        make(far, c + 2)

    each(0, 2, opposite)

    def near_beside(c):
        across(left, c, 4 + c).wait_recv()
        across(right, c, 8 + c).wait_recv()
        make(sibling + left - s, c)
        make(sibling + right - s, c)

    each(0, 4, near_beside)

    def far_beside(c):
        across(far, c, 12 + c).wait_recv()
        across(far, c + 2, 14 + c).wait_recv()
        make(sibling + far - s, c)
        make(sibling + far - s, c + 2)

    each(0, 2, far_beside)

    count = 4

    def center(m):
        for half in range(count):
            d = count * m + half
            values = grad[d * WIDE : d * WIDE + samples, :]
            mean = jnp.sum(values, axis=0, keepdims=True) * (1.0 / samples)
            cent[:, d * 128 : (d + 1) * 128] = ((values - mean) * norm_scale).astype(BF16)

    def store(m):
        at = pl.ds(m * 128 * count, 128 * count)
        return pltpu.make_async_copy(cent.at[:, at], cent_out.at[:, at], outs.at[m])

    def add(m):
        block = cent[:, m * 128 * count : (m + 1) * 128 * count]
        low = lax.dot_general(block, block[:256], (((1,), (1,)), ((), ())), preferred_element_type=F32)
        high = lax.dot_general(block[256:], block[256:], (((1,), (1,)), ((), ())), preferred_element_type=F32)
        for a, b, term in [(0, 512, low[:, :128]), (512, 896, low[128:, 128:]), (896, 1152, high[:, :128]), (1152, 1280, high[128:, 128:])]:
            if m == 0:
                part_ref[a:b, :] = term
            else:
                part_ref[a:b, :] += term

    steps = dims // count
    center(0)
    store(0).start()
    for m in range(1, steps):
        center(m)
        store(m).start()
        add(m - 1)
    add(steps - 1)

    core = lax.rem(s, 2)
    x = s // 2

    def slot(half, q):
        return pl.ds(pl.multiple_of(640 * half + 40 * q, 8), 40)

    give = pl.ds(pl.multiple_of(640 * (1 - core), 640), 640)
    keeps = pl.ds(pl.multiple_of(640 * core, 640), 640)
    copy = remote(part_ref.at[give], twin, s0.at[0], r0.at[0], (sibling, p))
    copy.wait_recv()
    part_ref[keeps, :] += twin[...]
    copies = [remote(part_ref.at[slot(core, q)], first.at[p], s1.at[k], r1.at[k], (s, q)) for k, q in enumerate(pars)]
    first[p] = part_ref[slot(core, p), :]
    for each_copy in copies:
        each_copy.wait_recv()
    total = first[0]
    for q in range(1, 16):
        total = total + first[q]
    second[x] = total
    more = [remote(second.at[x], second.at[x], s2.at[k], r2.at[k], (q, p)) for k, q in enumerate([right, far, left])]
    for each_copy in more:
        each_copy.wait_recv()
    total = second[0]
    for q in range(1, 4):
        total = total + second[q]
    gram_ref[slot(core, p), :] = total
    here = gram_ref.at[slot(core, p)]
    spread = [remote(here, here, s3.at[k], r3.at[k], (s, q)) for k, q in enumerate(pars)]
    passed = [remote(here, here, s4.at[15], r4.at[15], (sibling, p))]
    for k in range(15):
        spread[k].wait_recv()
        there = gram_ref.at[slot(core, lax.rem(p + 15 - k, 16))]
        passed.append(remote(there, there, s4.at[k], r4.at[k], (sibling, p)))
    for each_copy in passed:
        each_copy.wait()
    copy.wait_send()
    for each_copy in copies + more + spread:
        each_copy.wait_send()
    each(0, 4, lambda c: to_right(c).wait_send())
    each(0, 4, lambda c: to_left(c).wait_send())
    each(0, 2, lambda c: on_right(c).wait_send())
    each(0, 2, lambda c: on_left(c).wait_send())
    each(0, 16, lambda c: across(s, 0, c).wait_send())
    for m in range(steps):
        store(m).wait()


def gather_gram(ht_all, delta):
    sem = pltpu.SemaphoreType.DMA
    return pl.pallas_call(
        gather_gram_kernel,
        out_shape=[jax.ShapeDtypeStruct((512, 8192), BF16), jax.ShapeDtypeStruct((1280, 128), F32)],
        in_specs=[pl.BlockSpec(memory_space=pl.ANY)] * 2,
        out_specs=[pl.BlockSpec(memory_space=pl.ANY), pl.BlockSpec(memory_space=pltpu.VMEM)],
        scratch_shapes=[
            pltpu.VMEM((8, 16, 64, 128), BF16),
            pltpu.VMEM((8, 16, 112, 128), BF16),
            pltpu.VMEM((64 * WIDE, 128), F32),
            pltpu.VMEM((512, 8192), BF16),
            pltpu.VMEM((1280, 128), F32),
            pltpu.VMEM((640, 128), F32),
            pltpu.VMEM((16, 40, 128), F32),
            pltpu.VMEM((4, 40, 128), F32),
        ]
        + [sem((4,))] * 4
        + [sem((2,))] * 4
        + [sem((16,))] * 2
        + [sem((1,))] * 2
        + [sem((15,))] * 2
        + [sem((3,))] * 2
        + [sem((15,))] * 2
        + [sem((16,))] * 2
        + [sem((2,)), sem((16,))],
        compiler_params=pltpu.CompilerParams(collective_id=1, has_side_effects=True, vmem_limit_bytes=58 << 20),
        name="gather_gram",
    )(ht_all, delta)


def local_energy(spins, offdiag):
    side_sites = math.isqrt(spins.shape[1])
    spin_signs = (2 * spins - 1).astype(jnp.float32).reshape(spins.shape[0], side_sites, side_sites)
    right_spin = jnp.roll(spin_signs, -1, axis=2)
    down_spin = jnp.roll(spin_signs, -1, axis=1)
    diag_one = jnp.roll(down_spin, -1, axis=2)
    diag_two = jnp.roll(down_spin, 1, axis=2)
    near_bonds = jnp.sum(spin_signs * right_spin + spin_signs * down_spin, axis=(1, 2))
    far_bonds = jnp.sum(spin_signs * diag_one + spin_signs * diag_two, axis=(1, 2))
    return 0.25 * (near_bonds + SECOND_RATIO * far_bonds) + offdiag


def per_device(stream, weight_in, weight_out, readout, spins, offdiag):
    samples = spins.shape[0]
    norm_scale = 1.0 / math.sqrt(samples)
    ht_all, delta = forward(jnp.transpose(stream, (1, 0, 2)), weight_in, weight_out, readout[None, :])
    centered, gram = gather_gram(ht_all, delta)
    energies = local_energy(spins, offdiag)
    target = (energies - jnp.mean(energies)) * norm_scale
    return solve(gram, target[None, :], centered)


def solution(mesh):
    return jax.shard_map(
        per_device,
        mesh=mesh,
        in_specs=(P("samp", None, None), P("samp", "par"), P("par", None), P(), P(), P()),
        out_specs=P("samp", "par"),
        check_vma=False,
    )
```

```python
import functools
import math

import jax
import jax.numpy as jnp
from jax import lax
from jax.experimental import pallas as pl
from jax.experimental.pallas import tpu as pltpu
from jax.sharding import PartitionSpec as P

D = 512
FF = 2048
EPSILON = 1e-05
SHIFT_RATIO = 0.1
SECOND_RATIO = 0.5
MESH = pl.DeviceIdType.MESH
F32 = jnp.float32
BF16 = jnp.bfloat16
HI = lax.Precision.HIGHEST


def dot_nn(a, b):
    return lax.dot_general(a, b, (((1,), (0,)), ((), ())), precision=HI, preferred_element_type=F32)


def dot_nt(a, b):
    return lax.dot_general(a, b, (((1,), (1,)), ((), ())), precision=HI, preferred_element_type=F32)


def thirds(values):
    high = values.astype(BF16).astype(F32)
    rest = values - high
    middle = rest.astype(BF16).astype(F32)
    return high, middle, rest - middle


def outer(left, right):
    a, b, c = thirds(left)
    d, e, f = thirds(right)
    lhs = jnp.concatenate([a, a, b, a, b, c], axis=0).astype(BF16)
    rhs = jnp.concatenate([d, e, d, f, e, d], axis=0).astype(BF16)
    return lax.dot_general(lhs, rhs, (((0,), (0,)), ((), ())), preferred_element_type=F32)


def spread_column(values, at):
    return jnp.broadcast_to(values[:, at : at + 1], (8, 128))


def pick(values, row):
    return jnp.broadcast_to(values[row : row + 1, :], (8, 128))


def sweep_block(block):
    lane = lax.broadcasted_iota(jnp.int32, (8, 128), 1)
    sub = lax.broadcasted_iota(jnp.int32, (8, 128), 0)
    units = [jnp.where(sub == i, 1.0, 0.0) for i in range(8)]
    rows = [block[8 * r : 8 * r + 8, :] for r in range(16)]
    splat = [spread_column(rows[0], m) for m in range(8)]
    for g in range(16):
        panel = rows[g]
        before = panel
        last = g == 15
        ahead = [] if last else [spread_column(panel, 8 * g + 8 + m) for m in range(8)]
        old = [] if last else [spread_column(rows[g + 1], 8 * g + 8 + m) for m in range(8)]
        near = {r: [spread_column(rows[r], 8 * g + m) for m in range(8)] for r in (g + 1, g + 2) if r < 16}
        for i in range(8):
            factor = (splat[i] - units[i]) * (1.0 / pick(splat[i], i))
            panel = jnp.where(lane == 8 * g + i, units[i], panel)
            panel = panel - factor * pick(panel, i)
            for m in range(i + 1, 8):
                splat[m] = splat[m] - factor * pick(splat[m], i)
            ahead = [values - factor * pick(values, i) for values in ahead]
        if not last:
            splat = []
            for m in range(8):
                parts = [near[g + 1][j] * pick(ahead[m], j) for j in range(8)]
                even = (parts[0] + parts[2]) + (parts[4] + parts[6])
                odd = (parts[1] + parts[3]) + (parts[5] + parts[7])
                splat.append(old[m] - (even + odd))
        inside = (lane >= 8 * g) & (lane < 8 * g + 8)
        panel = jnp.where(inside, -panel, panel)
        change = outer(before, panel)
        spread = [pick(panel, m) for m in range(8)]
        for r in range(16):
            if r == g:
                continue
            kept = jnp.where(inside, 0.0, rows[r])
            if r in near:
                parts = [near[r][m] * spread[m] for m in range(8)]
                even = (parts[0] + parts[2]) + (parts[4] + parts[6])
                odd = (parts[1] + parts[3]) + (parts[5] + parts[7])
                rows[r] = kept - (even + odd)
            else:
                rows[r] = kept - change[8 * r : 8 * r + 8, :]
        rows[g] = panel
    return jnp.concatenate(rows, axis=0)


def solve_kernel(shift_ratio, scale, samples, gram_ref, target_ref, cent_hbm, out_ref, a_ref, w_ref, cent, sems):
    blocks = samples // 128
    chunks = sems.shape[0]
    wide = cent.shape[1] // chunks

    def load(m):
        at = pl.ds(m * wide, wide)
        return pltpu.make_async_copy(cent_hbm.at[:, at], cent.at[:, at], sems.at[m])

    for m in range(chunks):
        load(m).start()
    eye = lax.broadcasted_iota(jnp.int32, (128, 128), 0) == lax.broadcasted_iota(jnp.int32, (128, 128), 1)
    base = [0]
    for k in range(blocks):
        base.append(base[-1] + samples - 128 * k)
    trace = jnp.zeros((1, 1), F32)
    for k in range(blocks):
        trace += jnp.sum(jnp.where(eye, gram_ref[base[k] : base[k] + 128, :], 0.0), axis=(0, 1), keepdims=True)
    shift = shift_ratio * trace / samples
    shift = jnp.where(eye, jnp.broadcast_to(shift, (128, 128)), 0.0)
    rhs = []
    for k in range(blocks):
        a_ref[base[k] : base[k] + 128, :] = gram_ref[base[k] : base[k] + 128, :] + shift
        if k < blocks - 1:
            a_ref[base[k] + 128 : base[k + 1], :] = gram_ref[base[k] + 128 : base[k + 1], :]
        rhs.append(jnp.broadcast_to(target_ref[0:1, 128 * k : 128 * k + 128], (8, 128)))
    for k in range(blocks):
        inv = -sweep_block(a_ref[base[k] : base[k] + 128, :])
        if k < blocks - 1:
            below = a_ref[base[k] + 128 : base[k + 1], :]
            w = dot_nn(below, inv)
            w_ref[base[k] + 128 : base[k + 1], :] = w
            drop = dot_nt(rhs[k], w)
            for j in range(k + 1, blocks):
                at = 128 * (j - k - 1)
                a_ref[base[j] : base[j + 1], :] -= dot_nt(w[at:], below[at : at + 128])
                rhs[j] = rhs[j] - drop[:, at : at + 128]
        rhs[k] = dot_nn(rhs[k], inv)
    found = [None] * blocks
    for k in reversed(range(blocks)):
        x = rhs[k]
        for i in range(k + 1, blocks):
            r = base[k] + 128 * (i - k)
            x = x - dot_nn(found[i], w_ref[r : r + 128, :])
        found[k] = x
    coeffs = jnp.concatenate(found, axis=1).astype(BF16)
    for m in range(chunks):
        load(m).wait()
        part = jnp.dot(coeffs, cent[:, m * wide : (m + 1) * wide], preferred_element_type=F32) * scale
        for i in range(wide // 128):
            r = m * wide // 128 + i
            out_ref[r : r + 1, :] = part[0:1, 128 * i : 128 * (i + 1)]


def solve(gram, target, centered):
    samples, width = centered.shape
    blocks = samples // 128
    rows = blocks * (blocks + 1) // 2 * 128
    vmem = pl.BlockSpec(memory_space=pltpu.VMEM)
    return pl.pallas_call(
        functools.partial(solve_kernel, SHIFT_RATIO, -math.sqrt(D * FF), samples),
        out_shape=jax.ShapeDtypeStruct((width // 128, 128), F32),
        in_specs=[vmem, vmem, pl.BlockSpec(memory_space=pl.ANY)],
        out_specs=vmem,
        scratch_shapes=[
            pltpu.VMEM((rows, 128), F32),
            pltpu.VMEM((rows, 128), F32),
            pltpu.VMEM((samples, width), BF16),
            pltpu.SemaphoreType.DMA((8,)),
        ],
        compiler_params=pltpu.CompilerParams(vmem_limit_bytes=60 << 20),
        name="solve",
    )(gram, target, centered)


LSIDE = 10
GROUP = 4
WIDE = 8 * 65


def enter(ids):
    barrier = pltpu.get_barrier_semaphore()
    for device in ids:
        pl.semaphore_signal(barrier, inc=1, device_id=device, device_id_type=MESH)
    pl.semaphore_wait(barrier, len(ids))


def remote(src, dst, send, recv, device):
    copy = pltpu.make_async_remote_copy(
        src_ref=src, dst_ref=dst, send_sem=send, recv_sem=recv, device_id=device, device_id_type=MESH
    )
    copy.start()
    return copy


def describe(src, dst, send, recv, device):
    return pltpu.make_async_remote_copy(
        src_ref=src, dst_ref=dst, send_sem=send, recv_sem=recv, device_id=device, device_id_type=MESH
    )


def each(first, last, body):
    def step(k, carry):
        body(k)
        return carry

    lax.fori_loop(first, last, step, 0)


def make_target(spins_ref, offdiag_ref, norm_scale):
    signs = (2 * spins_ref[...] - 1).astype(F32)
    sites = signs.shape[0]
    column = lax.rem(lax.broadcasted_iota(jnp.int32, signs.shape, 0), LSIDE)

    def turn(values, by):
        return jnp.concatenate([values[by:], values[:by]], axis=0)

    def next_column(values):
        return jnp.where(column == LSIDE - 1, turn(values, sites - LSIDE + 1), turn(values, 1))

    def last_column(values):
        return jnp.where(column == 0, turn(values, LSIDE - 1), turn(values, sites - 1))

    down = turn(signs, LSIDE)
    near = jnp.sum(signs * (next_column(signs) + down), axis=0, keepdims=True)
    distant = jnp.sum(signs * (next_column(down) + last_column(down)), axis=0, keepdims=True)
    energies = 0.25 * (near + SECOND_RATIO * distant) + offdiag_ref[...]
    return (energies - jnp.mean(energies, axis=1, keepdims=True)) * norm_scale


def main_kernel(
    stream_ref, win_ref, wout_ref, readout_ref, spins_ref, offdiag_ref, cent_out, gram_ref, target_ref,
    win, wout, hid, ht, hall, slope, acc, dsend, dl, dall, grad, cent, part_ref, twin, first, second,
    xs, xr, ws, wr, vs, vr, wws, wwr, vvs, vvr, sws, swr, svs, svr, hs, hr, ls, lr,
    sr, rr, sl, rl, fr, qr, fl, ql, bs, br, s0, r0, s1, r1, s2, r2, s3, r3, s4, r4, own, outs,
):
    s, p = lax.axis_index("samp"), lax.axis_index("par")
    x, c = s // 2, lax.rem(s, 2)
    y, z = p // 4, lax.rem(p, 4)
    sibling = s + 1 - 2 * c
    n = 16
    groups, tokens = 16, 25
    rows, dims, width, samples = 112, 64, 128, 512
    norm_scale = 1.0 / math.sqrt(samples)
    right, left, far = lax.rem(s + 2, 8), lax.rem(s + 6, 8), lax.rem(s + 4, 8)
    pars = [lax.rem(p + k, 16) for k in range(1, 16)]
    enter([(s, lax.rem(p + k, n)) for k in range(1, n)] + [(lax.rem(s + k, 8), p) for k in range(1, 8)])

    def at(a, b):
        return lax.rem(y + a, 4) * 4 + lax.rem(z + b, 4)

    def origin(a, b):
        return at(4 - a, 4 - b)

    def xcopy(k):
        return describe(win_ref, win.at[p, x, c], xs.at[k - 1], xr.at[k - 1], (lax.rem(s + 2 * k, 8), p))

    def w_first(k):
        return describe(win.at[p, :, c], win.at[p, :, c], ws.at[k - 1], wr.at[k - 1], (s, at(k, 0)))

    def w_then(a, m):
        q, i = origin(a, 0), 3 * a + m - 1
        return describe(win.at[q, :, c], win.at[q, :, c], wws.at[i], wwr.at[i], (s, at(0, m)))

    def v_first(k):
        return describe(wout.at[p, c], wout.at[p, c], vs.at[k - 1], vr.at[k - 1], (s, at(0, k)))

    def v_then(b, m):
        q, i = origin(0, b), 3 * b + m - 1
        return describe(wout.at[q, c], wout.at[q, c], vvs.at[i], vvr.at[i], (s, at(m, 0)))

    def w_across(i):
        q = origin(i // 4, lax.rem(i, 4))
        return describe(win.at[q, :, c], win.at[q, :, c], sws.at[i], swr.at[i], (sibling, p))

    def v_across(i):
        q = origin(i // 4, lax.rem(i, 4))
        return describe(wout.at[q, c], wout.at[q, c], svs.at[i], svr.at[i], (sibling, p))

    def hcopy(k, c):
        to, at_c, i = lax.rem(s + k, 8), pl.ds(pl.multiple_of(4 * c, 4), 4), 4 * (k - 1) + c
        return describe(ht.at[to, at_c], hall.at[s, at_c], hs.at[i], hr.at[i], (to, p))

    def lcopy(k):
        q = lax.rem(p + k, n)
        return describe(dsend.at[q], dl.at[p], ls.at[k - 1], lr.at[k - 1], (s, q))

    mine_w = pltpu.make_async_copy(win_ref, win.at[p, x, c], own.at[0])
    mine_v = pltpu.make_async_copy(wout_ref.at[pl.ds(pl.multiple_of(64 * c, 64), 64)], wout.at[p, c], own.at[1])
    mine_w.start()
    mine_v.start()
    each(1, 4, lambda k: xcopy(k).start())
    mine_v.wait()
    each(1, 4, lambda k: v_first(k).start())
    each(1, 4, lambda m: v_then(0, m).start())
    v_across(0).start()
    mine_w.wait()

    def prepare(four):
        for v in range(2):
            pair = 2 * four + v
            values = stream_ref[:, pl.ds(pl.multiple_of(8 * pair, 8), 8), :]
            mean = jnp.mean(values, axis=-1, keepdims=True)
            centered = values - mean
            variance = jnp.mean(centered * centered, axis=-1, keepdims=True)
            scaled = centered * lax.rsqrt(variance + EPSILON)
            for half in range(2):
                u = 2 * v + half
                g = 4 * four + u
                pieces = [jnp.zeros((4 * u, 512), F32)] if u > 0 else []
                pieces += [scaled[t, 4 * half : 4 * half + 4] for t in range(tokens)]
                pieces += [jnp.zeros((width - 4 * tokens - 4 * u, 512), F32)]
                hidden = jnp.concatenate(pieces, axis=0)

                @pl.when(g == p)
                def _(hidden=hidden):
                    hid[...] = hidden[:rows].astype(BF16)

                flipped = jnp.transpose(hidden).astype(BF16)
                for q in range(8):
                    ht[q, g] = flipped[64 * q : 64 * (q + 1), :]

    def open_w():
        each(1, 4, lambda k: xcopy(k).wait_recv())
        each(1, 4, lambda k: w_first(k).start())
        each(1, 4, lambda m: w_then(0, m).start())
        w_across(0).start()

    def pass_v(k):
        v_first(k).wait_recv()
        each(1, 4, lambda m: v_then(k, m).start())
        v_across(k).start()

    def pass_w(k):
        w_first(k).wait_recv()
        each(1, 4, lambda m: w_then(k, m).start())
        w_across(4 * k).start()

    def work(step):
        @pl.when(step == 1)
        def _():
            each(1, 4, pass_v)

        @pl.when(step == 2)
        def _():
            each(1, 4, pass_w)

        prepare(step)
        each(1, 8, lambda k: hcopy(k, step).start())

        @pl.when(step == 0)
        def _():
            open_w()

    each(0, 4, work)
    mine_h = pltpu.make_async_copy(ht.at[s], hall.at[s], own.at[2])
    mine_h.start()
    target_ref[...] = make_target(spins_ref, offdiag_ref, norm_scale)
    acc[...] = jnp.zeros_like(acc)

    def take(a):
        for b in range(4):
            if b > 0:
                w_then(a, b).wait_recv()
                w_across(4 * a + b).start()

            @pl.when(a > 0)
            def _():
                v_then(b, a).wait_recv()
                v_across(4 * a + b).start()

    def compute(a):
        row = lax.rem(y - a + 4, 4)
        for b in range(4):
            w_across(4 * a + b).wait_recv()
            v_across(4 * a + b).wait_recv()
        weights = jnp.concatenate([win[4 * row + j].reshape(512, 128) for j in range(4)], axis=1)
        preact = jnp.dot(hid[...], weights, preferred_element_type=F32)
        active, pull = jax.vjp(jax.nn.gelu, preact)
        slope[row] = pull(jnp.ones_like(preact))[0]
        acc[...] += jnp.dot(active.astype(BF16), wout[pl.ds(4 * row, 4)].reshape(512, 512), preferred_element_type=F32)

    take(0)

    def both(a):
        take(a)
        compute(a - 1)

    each(1, 4, both)
    compute(3)
    signal = (readout_ref[...] * jnp.tanh(acc[...])).astype(BF16)

    def back(i):
        row = lax.rem(y + jnp.where(i < 2, i, 5 - i), 4)
        weights = wout[pl.ds(4 * row, 4)].reshape(512, 512)
        backward = lax.dot_general(signal, weights, (((1,), (1,)), ((), ())), preferred_element_type=F32)
        delta = (backward * slope[row]).astype(BF16)
        for j in range(4):
            q = 4 * row + j
            dsend[q] = delta[:, 128 * j : 128 * (j + 1)]

            @pl.when(q != p)
            def _():
                lcopy(lax.rem(q - p + n, n)).start()

    each(0, 4, back)
    dl[p] = dsend[p]

    def chunk(i):
        return lax.rem(y + jnp.where(i == 0, 0, jnp.where(i == 1, 3, i - 1)), 4)

    def move(origin, i, send, recv, device):
        part = dall.at[origin, chunk(i)]
        return describe(part, part, send, recv, device)

    def to_right(i):
        return move(s, i, sr.at[i], rr.at[i], (right, p))

    def to_left(i):
        return move(s, i, sl.at[i], rl.at[i], (left, p))

    def on_right(j):
        return move(left, 2 * j, fr.at[j], qr.at[j], (right, p))

    def on_left(j):
        return move(right, 2 * j + 1, fl.at[j], ql.at[j], (left, p))

    def across(origin, i, slot):
        return move(origin, i, bs.at[slot + i], br.at[slot + i], (sibling, p))

    def begin(i):
        f = chunk(i)
        for j in range(4):
            q = 4 * f + j

            @pl.when(q != p)
            def _(q=q):
                lcopy(lax.rem(p - q + n, n)).wait_recv()

        for u in range(4):
            window = dl[4 * f + u]
            dall[s, f, 96 * u + 16 : 96 * u + 96, :] = window[16:96]
            if u == 0:
                dall[s, f, 0:16, :] = window[0:16]
            else:
                dall[s, f, 96 * u : 96 * u + 16, :] = window[0:16] + dl[4 * f + u - 1][96:112]
            if u == 3:
                dall[s, f, 384:400, :] = window[96:112]
        to_right(i).start()
        to_left(i).start()
        across(s, i, 0).start()

    each(0, 4, begin)
    mine_h.wait()

    lane = lax.broadcasted_iota(jnp.int32, (dims, width), 1)
    keep = [lax.rem(lane, GROUP) == i for i in range(GROUP)]
    fill = jnp.zeros((width - rows, 128), BF16)
    nothing = jnp.zeros((dims, width), BF16)

    def make(origin, i):
        f = chunk(i)
        for u in range(4):
            group = 4 * f + u
            flipped = hall[origin, group]
            delta = jnp.concatenate([dall[origin, f, 96 * u : 96 * u + rows, :], fill], axis=0)
            stack = jnp.concatenate([jnp.where(keep[v], flipped, nothing) for v in range(GROUP)], axis=0)
            grads = jnp.dot(stack, delta, preferred_element_type=F32).astype(BF16).astype(F32)
            for v in range(GROUP):
                grad[pl.ds(64 * origin + GROUP * group + v, dims, stride=WIDE), :] = grads[dims * v : dims * (v + 1), :]

    each(0, 4, lambda i: make(s, i))
    each(1, 8, lambda k: each(0, 4, lambda f: hcopy(k, f).wait_recv()))

    def near(i):
        to_right(i).wait_recv()
        to_left(i).wait_recv()

        @pl.when(lax.rem(i, 2) == 0)
        def _():
            on_right(i // 2).start()

        @pl.when(lax.rem(i, 2) == 1)
        def _():
            on_left(i // 2).start()

        across(left, i, 4).start()
        across(right, i, 8).start()
        make(left, i)
        make(right, i)

    each(0, 4, near)

    def beside(i):
        across(s, i, 0).wait_recv()
        make(sibling, i)

    each(0, 4, beside)

    def opposite(j):
        on_right(j).wait_recv()
        across(far, 2 * j, 12).start()
        on_left(j).wait_recv()
        across(far, 2 * j + 1, 12).start()
        make(far, 2 * j)
        make(far, 2 * j + 1)

    each(0, 2, opposite)

    def near_beside(i):
        across(left, i, 4).wait_recv()
        across(right, i, 8).wait_recv()
        make(sibling + left - s, i)
        make(sibling + right - s, i)

    each(0, 4, near_beside)

    def far_beside(i):
        across(far, i, 12).wait_recv()
        make(sibling + far - s, i)

    each(0, 4, far_beside)

    count = 4

    def center(m):
        for half in range(count):
            d = count * m + half
            values = grad[d * WIDE : d * WIDE + samples, :]
            mean = jnp.sum(values, axis=0, keepdims=True) * (1.0 / samples)
            cent[:, d * 128 : (d + 1) * 128] = ((values - mean) * norm_scale).astype(BF16)

    def store(m):
        at = pl.ds(m * 128 * count, 128 * count)
        return pltpu.make_async_copy(cent.at[:, at], cent_out.at[:, at], outs.at[m])

    def add(m):
        block = cent[:, m * 128 * count : (m + 1) * 128 * count]
        low = lax.dot_general(block, block[:256], (((1,), (1,)), ((), ())), preferred_element_type=F32)
        high = lax.dot_general(block[256:], block[256:], (((1,), (1,)), ((), ())), preferred_element_type=F32)
        for a, b, term in [(0, 512, low[:, :128]), (512, 896, low[128:, 128:]), (896, 1152, high[:, :128]), (1152, 1280, high[128:, 128:])]:
            if m == 0:
                part_ref[a:b, :] = term
            else:
                part_ref[a:b, :] += term

    steps = dims // count
    center(0)
    store(0).start()
    for m in range(1, steps):
        center(m)
        store(m).start()
        add(m - 1)
    add(steps - 1)

    core = c

    def slot(half, q):
        return pl.ds(pl.multiple_of(640 * half + 40 * q, 8), 40)

    give = pl.ds(pl.multiple_of(640 * (1 - core), 640), 640)
    keeps = pl.ds(pl.multiple_of(640 * core, 640), 640)
    copy = remote(part_ref.at[give], twin, s0.at[0], r0.at[0], (sibling, p))
    copy.wait_recv()
    part_ref[keeps, :] += twin[...]
    copies = [remote(part_ref.at[slot(core, q)], first.at[p], s1.at[k], r1.at[k], (s, q)) for k, q in enumerate(pars)]
    first[p] = part_ref[slot(core, p), :]
    for each_copy in copies:
        each_copy.wait_recv()
    total = first[0]
    for q in range(1, 16):
        total = total + first[q]
    second[x] = total
    more = [remote(second.at[x], second.at[x], s2.at[k], r2.at[k], (q, p)) for k, q in enumerate([right, far, left])]
    for each_copy in more:
        each_copy.wait_recv()
    total = second[0]
    for q in range(1, 4):
        total = total + second[q]
    gram_ref[slot(core, p), :] = total
    here = gram_ref.at[slot(core, p)]
    spread = [remote(here, here, s3.at[k], r3.at[k], (s, q)) for k, q in enumerate(pars)]
    passed = [remote(here, here, s4.at[15], r4.at[15], (sibling, p))]
    for k in range(15):
        spread[k].wait_recv()
        there = gram_ref.at[slot(core, lax.rem(p + 15 - k, 16))]
        passed.append(remote(there, there, s4.at[k], r4.at[k], (sibling, p)))
    for each_copy in passed:
        each_copy.wait()
    copy.wait_send()
    for each_copy in copies + more + spread:
        each_copy.wait_send()
    each(0, 4, lambda c: to_right(c).wait_send())
    each(0, 4, lambda c: to_left(c).wait_send())
    each(0, 2, lambda c: on_right(c).wait_send())
    each(0, 2, lambda c: on_left(c).wait_send())
    each(0, 4, lambda i: each(0, 4, lambda j: across(s, i, 4 * j).wait_send()))
    for m in range(steps):
        store(m).wait()
    each(1, n, lambda k: lcopy(k).wait_send())
    each(1, 8, lambda k: each(0, 4, lambda c: hcopy(k, c).wait_send()))
    each(1, 4, lambda k: xcopy(k).wait_send())
    each(1, 4, lambda k: w_first(k).wait_send())
    each(1, 4, lambda k: v_first(k).wait_send())
    each(0, 4, lambda k: each(1, 4, lambda m: w_then(k, m).wait_send()))
    each(0, 4, lambda k: each(1, 4, lambda m: v_then(k, m).wait_send()))
    each(0, n, lambda i: w_across(i).wait_send())
    each(0, n, lambda i: v_across(i).wait_send())


def make_gram(stream, weight_in, weight_out, readout, spins, offdiag):
    rows = 112
    sem = pltpu.SemaphoreType.DMA
    vmem = pl.BlockSpec(memory_space=pltpu.VMEM)
    counts = [3, 3, 3, 12, 12, 16, 16, 28, 15, 4, 4, 2, 2, 16, 1, 15, 3, 15, 16]
    return pl.pallas_call(
        main_kernel,
        out_shape=[
            jax.ShapeDtypeStruct((512, 8192), BF16),
            jax.ShapeDtypeStruct((1280, 128), F32),
            jax.ShapeDtypeStruct((1, 512), F32),
        ],
        in_specs=[vmem] * 6,
        out_specs=[pl.BlockSpec(memory_space=pl.ANY), vmem, vmem],
        scratch_shapes=[
            pltpu.VMEM((16, 4, 2, 64, 128), BF16),
            pltpu.VMEM((16, 2, 64, 512), BF16),
            pltpu.VMEM((rows, 512), BF16),
            pltpu.VMEM((8, 16, 64, 128), BF16),
            pltpu.VMEM((8, 16, 64, 128), BF16),
            pltpu.VMEM((4, rows, 512), F32),
            pltpu.VMEM((rows, 512), F32),
            pltpu.VMEM((16, rows, 128), BF16),
            pltpu.VMEM((16, rows, 128), BF16),
            pltpu.VMEM((8, 4, 400, 128), BF16),
            pltpu.VMEM((64 * WIDE, 128), F32),
            pltpu.VMEM((512, 8192), BF16),
            pltpu.VMEM((1280, 128), F32),
            pltpu.VMEM((640, 128), F32),
            pltpu.VMEM((16, 40, 128), F32),
            pltpu.VMEM((4, 40, 128), F32),
        ]
        + [sem((count,)) for count in counts for _ in range(2)]
        + [sem((3,)), sem((16,))],
        compiler_params=pltpu.CompilerParams(collective_id=1, has_side_effects=True, vmem_limit_bytes=60 << 20),
        name="make_gram",
    )(stream, weight_in, weight_out, readout, spins, offdiag)


def per_device(stream, weight_in, weight_out, readout, spins, offdiag):
    centered, gram, target = make_gram(
        jnp.transpose(stream, (1, 0, 2)), weight_in, weight_out, readout[None, :], jnp.transpose(spins), offdiag[None, :]
    )
    return solve(gram, target, centered)


def solution(mesh):
    return jax.shard_map(
        per_device,
        mesh=mesh,
        in_specs=(P("samp", None, None), P("samp", "par"), P("par", None), P(), P(), P()),
        out_specs=P("samp", "par"),
        check_vma=False,
    )
```

```python
import functools
import math

import jax
import jax.numpy as jnp
from jax import lax
from jax.experimental import pallas as pl
from jax.experimental.pallas import tpu as pltpu
from jax.sharding import PartitionSpec as P

D = 512
FF = 2048
EPSILON = 1e-05
SHIFT_RATIO = 0.1
SECOND_RATIO = 0.5
MESH = pl.DeviceIdType.MESH
F32 = jnp.float32
BF16 = jnp.bfloat16
HI = lax.Precision.HIGHEST


def dot_nn(a, b):
    return lax.dot_general(a, b, (((1,), (0,)), ((), ())), precision=HI, preferred_element_type=F32)


def dot_nt(a, b):
    return lax.dot_general(a, b, (((1,), (1,)), ((), ())), precision=HI, preferred_element_type=F32)


def thirds(values):
    high = values.astype(BF16).astype(F32)
    rest = values - high
    middle = rest.astype(BF16).astype(F32)
    return high, middle, rest - middle


def outer(left, right):
    a, b, c = thirds(left)
    d, e, f = thirds(right)
    lhs = jnp.concatenate([a, a, b, a, b, c], axis=0).astype(BF16)
    rhs = jnp.concatenate([d, e, d, f, e, d], axis=0).astype(BF16)
    return lax.dot_general(lhs, rhs, (((0,), (0,)), ((), ())), preferred_element_type=F32)


def spread_column(values, at):
    return jnp.broadcast_to(values[:, at : at + 1], (8, 128))


def pick(values, row):
    return jnp.broadcast_to(values[row : row + 1, :], (8, 128))


def sweep_block(block, later):
    lane = lax.broadcasted_iota(jnp.int32, (8, 128), 1)
    sub = lax.broadcasted_iota(jnp.int32, (8, 128), 0)
    units = [jnp.where(sub == i, 1.0, 0.0) for i in range(8)]
    rows = [block[8 * r : 8 * r + 8, :] for r in range(16)]
    splat = [spread_column(rows[0], m) for m in range(8)]
    ahead = [spread_column(rows[0], 8 + m) for m in range(8)]
    for g in range(16):
        panel = rows[g]
        before = panel
        last = g == 15
        beyond = [spread_column(panel, 8 * g + 16 + m) for m in range(8)] if g < 14 else []
        old = [] if last else [spread_column(rows[g + 1], 8 * g + 8 + m) for m in range(16 if g < 14 else 8)]
        near = {r: [spread_column(rows[r], 8 * g + m) for m in range(8)] for r in (g + 1, g + 2) if r < 16}
        for i in range(8):
            factor = (splat[i] - units[i]) * (1.0 / pick(splat[i], i))
            panel = jnp.where(lane == 8 * g + i, units[i], panel)
            panel = panel - factor * pick(panel, i)
            for m in range(i + 1, 8):
                splat[m] = splat[m] - factor * pick(splat[m], i)
            ahead = [values - factor * pick(values, i) for values in ahead]
            beyond = [values - factor * pick(values, i) for values in beyond]
        if not last:
            fresh = []
            for m, values in enumerate(ahead + beyond):
                parts = [near[g + 1][j] * pick(values, j) for j in range(8)]
                even = (parts[0] + parts[2]) + (parts[4] + parts[6])
                odd = (parts[1] + parts[3]) + (parts[5] + parts[7])
                fresh.append(old[m] - (even + odd))
            splat, ahead = fresh[:8], fresh[8:]
        inside = (lane >= 8 * g) & (lane < 8 * g + 8)
        panel = jnp.where(inside, -panel, panel)
        change = outer(before, panel)
        spread = [pick(panel, m) for m in range(8)]
        for r in range(16):
            if r == g:
                continue
            kept = jnp.where(inside, 0.0, rows[r])
            if r in near:
                parts = [near[r][m] * spread[m] for m in range(8)]
                even = (parts[0] + parts[2]) + (parts[4] + parts[6])
                odd = (parts[1] + parts[3]) + (parts[5] + parts[7])
                rows[r] = kept - (even + odd)
            else:
                rows[r] = kept - change[8 * r : 8 * r + 8, :]
        rows[g] = panel
        if later:
            later.pop(0)()
    while later:
        later.pop(0)()
    return jnp.concatenate(rows, axis=0)


def solve_kernel(shift_ratio, scale, samples, gram_ref, target_ref, cent_hbm, out_ref, cent, sems):
    blocks = samples // 128
    chunks = sems.shape[0]
    wide = cent.shape[1] // chunks

    def load(m):
        at = pl.ds(m * wide, wide)
        return pltpu.make_async_copy(cent_hbm.at[:, at], cent.at[:, at], sems.at[m])

    for m in range(chunks):
        load(m).start()
    eye = lax.broadcasted_iota(jnp.int32, (128, 128), 0) == lax.broadcasted_iota(jnp.int32, (128, 128), 1)
    base = [0]
    for k in range(blocks):
        base.append(base[-1] + samples - 128 * k)
    trace = jnp.zeros((1, 1), F32)
    for k in range(blocks):
        trace += jnp.sum(jnp.where(eye, gram_ref[base[k] : base[k] + 128, :], 0.0), axis=(0, 1), keepdims=True)
    shift = shift_ratio * trace / samples
    shift = jnp.where(eye, jnp.broadcast_to(shift, (128, 128)), 0.0)
    rhs = []
    tiles, quot = {}, {}
    for k in range(blocks):
        for i in range(k, blocks):
            at = base[k] + 128 * (i - k)
            tiles[i, k] = gram_ref[at : at + 128, :] + shift if i == k else gram_ref[at : at + 128, :]
        rhs.append(jnp.broadcast_to(target_ref[0:1, 128 * k : 128 * k + 128], (8, 128)))

    def divide(i, k, inv):
        def run():
            quot[i, k] = dot_nn(tiles[i, k], inv)

        return run

    def reduce(i, j, k):
        def run():
            tiles[i, j] = tiles[i, j] - dot_nt(quot[i, k], tiles[j, k])

        return run

    def lower(i, k, right):
        def run():
            rhs[i] = rhs[i] - dot_nt(right, quot[i, k])

        return run

    def close(k, right, inv):
        def run():
            rhs[k] = dot_nn(right, inv)

        return run

    later = []
    for k in range(blocks):
        inv = -sweep_block(tiles[k, k], later)
        later = []
        if k < blocks - 1:
            divide(k + 1, k, inv)()
            reduce(k + 1, k + 1, k)()
            later += [divide(i, k, inv) for i in range(k + 2, blocks)]
            later += [reduce(i, k + 1, k) for i in range(k + 2, blocks)]
            later += [reduce(i, j, k) for j in range(k + 2, blocks) for i in range(j, blocks)]
            later += [lower(i, k, rhs[k]) for i in range(k + 1, blocks)]
        if k < blocks - 1:
            later.append(close(k, rhs[k], inv))
        else:
            close(k, rhs[k], inv)()
    found = [None] * blocks
    for k in reversed(range(blocks)):
        x = rhs[k]
        for i in range(k + 1, blocks):
            x = x - dot_nn(found[i], quot[i, k])
        found[k] = x
    coeffs = jnp.concatenate(found, axis=1).astype(BF16)
    for m in range(chunks):
        load(m).wait()
        part = jnp.dot(coeffs, cent[:, m * wide : (m + 1) * wide], preferred_element_type=F32) * scale
        for i in range(wide // 128):
            r = m * wide // 128 + i
            out_ref[r : r + 1, :] = part[0:1, 128 * i : 128 * (i + 1)]


def solve(gram, target, centered):
    samples, width = centered.shape
    blocks = samples // 128
    vmem = pl.BlockSpec(memory_space=pltpu.VMEM)
    return pl.pallas_call(
        functools.partial(solve_kernel, SHIFT_RATIO, -math.sqrt(D * FF), samples),
        out_shape=jax.ShapeDtypeStruct((width // 128, 128), F32),
        in_specs=[vmem, vmem, pl.BlockSpec(memory_space=pl.ANY)],
        out_specs=vmem,
        scratch_shapes=[
            pltpu.VMEM((samples, width), BF16),
            pltpu.SemaphoreType.DMA((8,)),
        ],
        compiler_params=pltpu.CompilerParams(vmem_limit_bytes=60 << 20),
        name="solve",
    )(gram, target, centered)


LSIDE = 10
GROUP = 4
WIDE = 8 * 65


def enter(ids):
    barrier = pltpu.get_barrier_semaphore()
    for device in ids:
        pl.semaphore_signal(barrier, inc=1, device_id=device, device_id_type=MESH)
    pl.semaphore_wait(barrier, len(ids))


def remote(src, dst, send, recv, device):
    copy = pltpu.make_async_remote_copy(
        src_ref=src, dst_ref=dst, send_sem=send, recv_sem=recv, device_id=device, device_id_type=MESH
    )
    copy.start()
    return copy


def describe(src, dst, send, recv, device):
    return pltpu.make_async_remote_copy(
        src_ref=src, dst_ref=dst, send_sem=send, recv_sem=recv, device_id=device, device_id_type=MESH
    )


def each(first, last, body):
    def step(k, carry):
        body(k)
        return carry

    lax.fori_loop(first, last, step, 0)


def make_target(spins_ref, offdiag_ref, norm_scale):
    signs = (2 * spins_ref[...] - 1).astype(F32)
    sites = signs.shape[0]
    column = lax.rem(lax.broadcasted_iota(jnp.int32, signs.shape, 0), LSIDE)

    def turn(values, by):
        return jnp.concatenate([values[by:], values[:by]], axis=0)

    def next_column(values):
        return jnp.where(column == LSIDE - 1, turn(values, sites - LSIDE + 1), turn(values, 1))

    def last_column(values):
        return jnp.where(column == 0, turn(values, LSIDE - 1), turn(values, sites - 1))

    down = turn(signs, LSIDE)
    near = jnp.sum(signs * (next_column(signs) + down), axis=0, keepdims=True)
    distant = jnp.sum(signs * (next_column(down) + last_column(down)), axis=0, keepdims=True)
    energies = 0.25 * (near + SECOND_RATIO * distant) + offdiag_ref[...]
    return (energies - jnp.mean(energies, axis=1, keepdims=True)) * norm_scale


def main_kernel(
    stream_ref, win_ref, wout_ref, readout_ref, spins_ref, offdiag_ref, cent_out, gram_ref, target_ref,
    win, wout, hid, ht, hall, slope, acc, dsend, dl, dall, grad, cent, part_ref, twin, first, second,
    xs, xr, ws, wr, vs, vr, wws, wwr, vvs, vvr, sws, swr, svs, svr, hs, hr, ls, lr,
    sr, rr, sl, rl, fr, qr, fl, ql, bs, br, s0, r0, s1, r1, s2, r2, s3, r3, s4, r4, own, outs,
):
    s, p = lax.axis_index("samp"), lax.axis_index("par")
    x, c = s // 2, lax.rem(s, 2)
    y, z = p // 4, lax.rem(p, 4)
    sibling = s + 1 - 2 * c
    n = 16
    groups, tokens = 16, 25
    rows, dims, width, samples = 112, 64, 128, 512
    norm_scale = 1.0 / math.sqrt(samples)
    right, left, far = lax.rem(s + 2, 8), lax.rem(s + 6, 8), lax.rem(s + 4, 8)
    pars = [lax.rem(p + k, 16) for k in range(1, 16)]
    enter([(s, lax.rem(p + k, n)) for k in range(1, n)] + [(lax.rem(s + k, 8), p) for k in range(1, 8)])

    def at(a, b):
        return lax.rem(y + a, 4) * 4 + lax.rem(z + b, 4)

    def origin(a, b):
        return at(4 - a, 4 - b)

    def xcopy(k):
        return describe(win_ref, win.at[p, x, c], xs.at[k - 1], xr.at[k - 1], (lax.rem(s + 2 * k, 8), p))

    def w_first(k):
        return describe(win.at[p, :, c], win.at[p, :, c], ws.at[k - 1], wr.at[k - 1], (s, at(k, 0)))

    def w_then(a, m):
        q, i = origin(a, 0), 3 * a + m - 1
        return describe(win.at[q, :, c], win.at[q, :, c], wws.at[i], wwr.at[i], (s, at(0, m)))

    def v_first(k):
        return describe(wout.at[p, c], wout.at[p, c], vs.at[k - 1], vr.at[k - 1], (s, at(0, k)))

    def v_then(b, m):
        q, i = origin(0, b), 3 * b + m - 1
        return describe(wout.at[q, c], wout.at[q, c], vvs.at[i], vvr.at[i], (s, at(m, 0)))

    def w_across(i):
        q = origin(i // 4, lax.rem(i, 4))
        return describe(win.at[q, :, c], win.at[q, :, c], sws.at[i], swr.at[i], (sibling, p))

    def v_across(i):
        q = origin(i // 4, lax.rem(i, 4))
        return describe(wout.at[q, c], wout.at[q, c], svs.at[i], svr.at[i], (sibling, p))

    def hcopy(k, c):
        to, at_c, i = lax.rem(s + k, 8), pl.ds(pl.multiple_of(4 * c, 4), 4), 4 * (k - 1) + c
        return describe(ht.at[to, at_c], hall.at[s, at_c], hs.at[i], hr.at[i], (to, p))

    def lcopy(k):
        q = lax.rem(p + k, n)
        return describe(dsend.at[q], dl.at[p], ls.at[k - 1], lr.at[k - 1], (s, q))

    mine_w = pltpu.make_async_copy(win_ref, win.at[p, x, c], own.at[0])
    mine_v = pltpu.make_async_copy(wout_ref.at[pl.ds(pl.multiple_of(64 * c, 64), 64)], wout.at[p, c], own.at[1])
    mine_w.start()
    mine_v.start()
    each(1, 4, lambda k: xcopy(k).start())
    mine_v.wait()
    each(1, 4, lambda k: v_first(k).start())
    each(1, 4, lambda m: v_then(0, m).start())
    v_across(0).start()
    mine_w.wait()

    def prepare(four):
        for v in range(2):
            pair = 2 * four + v
            values = stream_ref[:, pl.ds(pl.multiple_of(8 * pair, 8), 8), :]
            mean = jnp.mean(values, axis=-1, keepdims=True)
            centered = values - mean
            variance = jnp.mean(centered * centered, axis=-1, keepdims=True)
            scaled = centered * lax.rsqrt(variance + EPSILON)
            for half in range(2):
                u = 2 * v + half
                g = 4 * four + u
                pieces = [jnp.zeros((4 * u, 512), F32)] if u > 0 else []
                pieces += [scaled[t, 4 * half : 4 * half + 4] for t in range(tokens)]
                pieces += [jnp.zeros((width - 4 * tokens - 4 * u, 512), F32)]
                hidden = jnp.concatenate(pieces, axis=0)

                @pl.when(g == p)
                def _(hidden=hidden):
                    hid[...] = hidden[:rows].astype(BF16)

                flipped = jnp.transpose(hidden).astype(BF16)
                for q in range(8):
                    ht[q, g] = flipped[64 * q : 64 * (q + 1), :]

    def open_w():
        each(1, 4, lambda k: xcopy(k).wait_recv())
        each(1, 4, lambda k: w_first(k).start())
        each(1, 4, lambda m: w_then(0, m).start())
        w_across(0).start()

    def pass_v(k):
        v_first(k).wait_recv()
        each(1, 4, lambda m: v_then(k, m).start())
        v_across(k).start()

    def pass_w(k):
        w_first(k).wait_recv()
        each(1, 4, lambda m: w_then(k, m).start())
        w_across(4 * k).start()

    def work(step):
        @pl.when(step == 1)
        def _():
            each(1, 4, pass_v)

        @pl.when(step == 2)
        def _():
            each(1, 4, pass_w)

        prepare(step)
        each(1, 8, lambda k: hcopy(k, step).start())

        @pl.when(step == 0)
        def _():
            open_w()

    each(0, 4, work)
    mine_h = pltpu.make_async_copy(ht.at[s], hall.at[s], own.at[2])
    mine_h.start()
    target_ref[...] = make_target(spins_ref, offdiag_ref, norm_scale)
    acc[...] = jnp.zeros_like(acc)

    def take(a):
        for b in range(4):
            if b > 0:
                w_then(a, b).wait_recv()
                w_across(4 * a + b).start()

            @pl.when(a > 0)
            def _():
                v_then(b, a).wait_recv()
                v_across(4 * a + b).start()

    def compute(a):
        row = lax.rem(y - a + 4, 4)
        for b in range(4):
            w_across(4 * a + b).wait_recv()
            v_across(4 * a + b).wait_recv()
        weights = jnp.concatenate([win[4 * row + j].reshape(512, 128) for j in range(4)], axis=1)
        preact = jnp.dot(hid[...], weights, preferred_element_type=F32)
        active, pull = jax.vjp(jax.nn.gelu, preact)
        slope[row] = pull(jnp.ones_like(preact))[0]
        acc[...] += jnp.dot(active.astype(BF16), wout[pl.ds(4 * row, 4)].reshape(512, 512), preferred_element_type=F32)

    take(0)

    def both(a):
        take(a)
        compute(a - 1)

    each(1, 4, both)
    compute(3)
    signal = (readout_ref[...] * jnp.tanh(acc[...])).astype(BF16)

    def back(i):
        row = lax.rem(y + jnp.where(i < 2, i, 5 - i), 4)
        weights = wout[pl.ds(4 * row, 4)].reshape(512, 512)
        backward = lax.dot_general(signal, weights, (((1,), (1,)), ((), ())), preferred_element_type=F32)
        delta = (backward * slope[row]).astype(BF16)
        for j in range(4):
            q = 4 * row + j
            dsend[q] = delta[:, 128 * j : 128 * (j + 1)]

            @pl.when(q != p)
            def _():
                lcopy(lax.rem(q - p + n, n)).start()

    each(0, 4, back)
    dl[p] = dsend[p]

    def chunk(i):
        return lax.rem(y + jnp.where(i == 0, 0, jnp.where(i == 1, 3, i - 1)), 4)

    def move(origin, i, send, recv, device):
        part = dall.at[origin, chunk(i)]
        return describe(part, part, send, recv, device)

    def to_right(i):
        return move(s, i, sr.at[i], rr.at[i], (right, p))

    def to_left(i):
        return move(s, i, sl.at[i], rl.at[i], (left, p))

    def on_right(j):
        return move(left, 2 * j, fr.at[j], qr.at[j], (right, p))

    def on_left(j):
        return move(right, 2 * j + 1, fl.at[j], ql.at[j], (left, p))

    def across(origin, i, slot):
        return move(origin, i, bs.at[slot + i], br.at[slot + i], (sibling, p))

    def begin(i):
        f = chunk(i)
        for j in range(4):
            q = 4 * f + j

            @pl.when(q != p)
            def _(q=q):
                lcopy(lax.rem(p - q + n, n)).wait_recv()

        for u in range(4):
            window = dl[4 * f + u]
            dall[s, f, 96 * u + 16 : 96 * u + 96, :] = window[16:96]
            if u == 0:
                dall[s, f, 0:16, :] = window[0:16]
            else:
                dall[s, f, 96 * u : 96 * u + 16, :] = window[0:16] + dl[4 * f + u - 1][96:112]
            if u == 3:
                dall[s, f, 384:400, :] = window[96:112]
        to_right(i).start()
        to_left(i).start()
        across(s, i, 0).start()

    each(0, 4, begin)
    mine_h.wait()

    lane = lax.broadcasted_iota(jnp.int32, (dims, width), 1)
    keep = [lax.rem(lane, GROUP) == i for i in range(GROUP)]
    fill = jnp.zeros((width - rows, 128), BF16)
    nothing = jnp.zeros((dims, width), BF16)

    def make(origin, i):
        f = chunk(i)
        for u in range(4):
            group = 4 * f + u
            flipped = hall[origin, group]
            delta = jnp.concatenate([dall[origin, f, 96 * u : 96 * u + rows, :], fill], axis=0)
            stack = jnp.concatenate([jnp.where(keep[v], flipped, nothing) for v in range(GROUP)], axis=0)
            grads = jnp.dot(stack, delta, preferred_element_type=F32).astype(BF16).astype(F32)
            for v in range(GROUP):
                grad[pl.ds(64 * origin + GROUP * group + v, dims, stride=WIDE), :] = grads[dims * v : dims * (v + 1), :]

    each(0, 4, lambda i: make(s, i))
    each(1, 8, lambda k: each(0, 4, lambda f: hcopy(k, f).wait_recv()))

    def near(i):
        to_right(i).wait_recv()
        to_left(i).wait_recv()

        @pl.when(lax.rem(i, 2) == 0)
        def _():
            on_right(i // 2).start()

        @pl.when(lax.rem(i, 2) == 1)
        def _():
            on_left(i // 2).start()

        across(left, i, 4).start()
        across(right, i, 8).start()
        make(left, i)
        make(right, i)

    each(0, 4, near)

    def beside(i):
        across(s, i, 0).wait_recv()
        make(sibling, i)

    each(0, 4, beside)

    def opposite(j):
        on_right(j).wait_recv()
        across(far, 2 * j, 12).start()
        on_left(j).wait_recv()
        across(far, 2 * j + 1, 12).start()
        make(far, 2 * j)
        make(far, 2 * j + 1)

    each(0, 2, opposite)

    def near_beside(i):
        across(left, i, 4).wait_recv()
        across(right, i, 8).wait_recv()
        make(sibling + left - s, i)
        make(sibling + right - s, i)

    each(0, 4, near_beside)

    def far_beside(i):
        across(far, i, 12).wait_recv()
        make(sibling + far - s, i)

    each(0, 4, far_beside)

    count = 4

    def center(m):
        for half in range(count):
            d = count * m + half
            values = grad[d * WIDE : d * WIDE + samples, :]
            mean = jnp.sum(values, axis=0, keepdims=True) * (1.0 / samples)
            cent[:, d * 128 : (d + 1) * 128] = ((values - mean) * norm_scale).astype(BF16)

    def store(m):
        at = pl.ds(m * 128 * count, 128 * count)
        return pltpu.make_async_copy(cent.at[:, at], cent_out.at[:, at], outs.at[m])

    def add(m):
        block = cent[:, m * 128 * count : (m + 1) * 128 * count]
        low = lax.dot_general(block, block[:256], (((1,), (1,)), ((), ())), preferred_element_type=F32)
        high = lax.dot_general(block[256:], block[256:], (((1,), (1,)), ((), ())), preferred_element_type=F32)
        for a, b, term in [(0, 512, low[:, :128]), (512, 896, low[128:, 128:]), (896, 1152, high[:, :128]), (1152, 1280, high[128:, 128:])]:
            if m == 0:
                part_ref[a:b, :] = term
            else:
                part_ref[a:b, :] += term

    steps = dims // count
    center(0)
    store(0).start()
    for m in range(1, steps):
        center(m)
        store(m).start()
        add(m - 1)
    add(steps - 1)

    core = c

    def slot(half, q):
        return pl.ds(pl.multiple_of(640 * half + 40 * q, 8), 40)

    give = pl.ds(pl.multiple_of(640 * (1 - core), 640), 640)
    keeps = pl.ds(pl.multiple_of(640 * core, 640), 640)
    copy = remote(part_ref.at[give], twin, s0.at[0], r0.at[0], (sibling, p))
    copy.wait_recv()
    part_ref[keeps, :] += twin[...]
    copies = [remote(part_ref.at[slot(core, q)], first.at[p], s1.at[k], r1.at[k], (s, q)) for k, q in enumerate(pars)]
    first[p] = part_ref[slot(core, p), :]
    for each_copy in copies:
        each_copy.wait_recv()
    total = first[0]
    for q in range(1, 16):
        total = total + first[q]
    second[x] = total
    more = [remote(second.at[x], second.at[x], s2.at[k], r2.at[k], (q, p)) for k, q in enumerate([right, far, left])]
    for each_copy in more:
        each_copy.wait_recv()
    total = second[0]
    for q in range(1, 4):
        total = total + second[q]
    gram_ref[slot(core, p), :] = total
    here = gram_ref.at[slot(core, p)]
    spread = [remote(here, here, s3.at[k], r3.at[k], (s, q)) for k, q in enumerate(pars)]
    passed = [remote(here, here, s4.at[15], r4.at[15], (sibling, p))]
    for k in range(15):
        spread[k].wait_recv()
        there = gram_ref.at[slot(core, lax.rem(p + 15 - k, 16))]
        passed.append(remote(there, there, s4.at[k], r4.at[k], (sibling, p)))
    for each_copy in passed:
        each_copy.wait()
    copy.wait_send()
    for each_copy in copies + more + spread:
        each_copy.wait_send()
    each(0, 4, lambda c: to_right(c).wait_send())
    each(0, 4, lambda c: to_left(c).wait_send())
    each(0, 2, lambda c: on_right(c).wait_send())
    each(0, 2, lambda c: on_left(c).wait_send())
    each(0, 4, lambda i: each(0, 4, lambda j: across(s, i, 4 * j).wait_send()))
    for m in range(steps):
        store(m).wait()
    each(1, n, lambda k: lcopy(k).wait_send())
    each(1, 8, lambda k: each(0, 4, lambda c: hcopy(k, c).wait_send()))
    each(1, 4, lambda k: xcopy(k).wait_send())
    each(1, 4, lambda k: w_first(k).wait_send())
    each(1, 4, lambda k: v_first(k).wait_send())
    each(0, 4, lambda k: each(1, 4, lambda m: w_then(k, m).wait_send()))
    each(0, 4, lambda k: each(1, 4, lambda m: v_then(k, m).wait_send()))
    each(0, n, lambda i: w_across(i).wait_send())
    each(0, n, lambda i: v_across(i).wait_send())


def make_gram(stream, weight_in, weight_out, readout, spins, offdiag):
    rows = 112
    sem = pltpu.SemaphoreType.DMA
    vmem = pl.BlockSpec(memory_space=pltpu.VMEM)
    counts = [3, 3, 3, 12, 12, 16, 16, 28, 15, 4, 4, 2, 2, 16, 1, 15, 3, 15, 16]
    return pl.pallas_call(
        main_kernel,
        out_shape=[
            jax.ShapeDtypeStruct((512, 8192), BF16),
            jax.ShapeDtypeStruct((1280, 128), F32),
            jax.ShapeDtypeStruct((1, 512), F32),
        ],
        in_specs=[vmem] * 6,
        out_specs=[pl.BlockSpec(memory_space=pl.ANY), vmem, vmem],
        scratch_shapes=[
            pltpu.VMEM((16, 4, 2, 64, 128), BF16),
            pltpu.VMEM((16, 2, 64, 512), BF16),
            pltpu.VMEM((rows, 512), BF16),
            pltpu.VMEM((8, 16, 64, 128), BF16),
            pltpu.VMEM((8, 16, 64, 128), BF16),
            pltpu.VMEM((4, rows, 512), F32),
            pltpu.VMEM((rows, 512), F32),
            pltpu.VMEM((16, rows, 128), BF16),
            pltpu.VMEM((16, rows, 128), BF16),
            pltpu.VMEM((8, 4, 400, 128), BF16),
            pltpu.VMEM((64 * WIDE, 128), F32),
            pltpu.VMEM((512, 8192), BF16),
            pltpu.VMEM((1280, 128), F32),
            pltpu.VMEM((640, 128), F32),
            pltpu.VMEM((16, 40, 128), F32),
            pltpu.VMEM((4, 40, 128), F32),
        ]
        + [sem((count,)) for count in counts for _ in range(2)]
        + [sem((3,)), sem((16,))],
        compiler_params=pltpu.CompilerParams(collective_id=1, has_side_effects=True, vmem_limit_bytes=60 << 20),
        name="make_gram",
    )(stream, weight_in, weight_out, readout, spins, offdiag)


def per_device(stream, weight_in, weight_out, readout, spins, offdiag):
    centered, gram, target = make_gram(
        jnp.transpose(stream, (1, 0, 2)), weight_in, weight_out, readout[None, :], jnp.transpose(spins), offdiag[None, :]
    )
    return solve(gram, target, centered)


def solution(mesh):
    return jax.shard_map(
        per_device,
        mesh=mesh,
        in_specs=(P("samp", None, None), P("samp", "par"), P("par", None), P(), P(), P()),
        out_specs=P("samp", "par"),
        check_vma=False,
    )
```

```python
import functools
import math

import jax
import jax.numpy as jnp
from jax import lax
from jax.experimental import pallas as pl
from jax.experimental.pallas import tpu as pltpu
from jax.sharding import PartitionSpec as P

D = 512
FF = 2048
EPSILON = 1e-05
SHIFT_RATIO = 0.1
SECOND_RATIO = 0.5
MESH = pl.DeviceIdType.MESH
F32 = jnp.float32
BF16 = jnp.bfloat16
HI = lax.Precision.HIGHEST


def dot_nn(a, b):
    return lax.dot_general(a, b, (((1,), (0,)), ((), ())), precision=HI, preferred_element_type=F32)


def dot_nt(a, b):
    return lax.dot_general(a, b, (((1,), (1,)), ((), ())), precision=HI, preferred_element_type=F32)


def thirds(values):
    high = values.astype(BF16).astype(F32)
    rest = values - high
    middle = rest.astype(BF16).astype(F32)
    return high, middle, rest - middle


def outer(left, right):
    a, b, c = thirds(left)
    d, e, f = thirds(right)
    lhs = jnp.concatenate([a, a, b, a, b, c], axis=0).astype(BF16)
    rhs = jnp.concatenate([d, e, d, f, e, d], axis=0).astype(BF16)
    return lax.dot_general(lhs, rhs, (((0,), (0,)), ((), ())), preferred_element_type=F32)


def spread_column(values, at):
    return jnp.broadcast_to(values[:, at : at + 1], (8, 128))


def pick(values, row):
    return jnp.broadcast_to(values[row : row + 1, :], (8, 128))


def sweep_block(block, later):
    lane = lax.broadcasted_iota(jnp.int32, (8, 128), 1)
    sub = lax.broadcasted_iota(jnp.int32, (8, 128), 0)
    units = [jnp.where(sub == i, 1.0, 0.0) for i in range(8)]
    rows = [block[8 * r : 8 * r + 8, :] for r in range(16)]
    splat = [spread_column(rows[0], m) for m in range(8)]
    ahead = [spread_column(rows[0], 8 + m) for m in range(8)]
    for g in range(16):
        panel = rows[g]
        before = panel
        last = g == 15
        beyond = [spread_column(panel, 8 * g + 16 + m) for m in range(8)] if g < 14 else []
        old = [] if last else [spread_column(rows[g + 1], 8 * g + 8 + m) for m in range(16 if g < 14 else 8)]
        near = {r: [spread_column(rows[r], 8 * g + m) for m in range(8)] for r in (g + 1, g + 2) if r < 16}
        for i in range(8):
            factor = (splat[i] - units[i]) * (1.0 / pick(splat[i], i))
            panel = jnp.where(lane == 8 * g + i, units[i], panel)
            panel = panel - factor * pick(panel, i)
            for m in range(i + 1, 8):
                splat[m] = splat[m] - factor * pick(splat[m], i)
            ahead = [values - factor * pick(values, i) for values in ahead]
            beyond = [values - factor * pick(values, i) for values in beyond]
        if not last:
            fresh = []
            for m, values in enumerate(ahead + beyond):
                parts = [near[g + 1][j] * pick(values, j) for j in range(8)]
                even = (parts[0] + parts[2]) + (parts[4] + parts[6])
                odd = (parts[1] + parts[3]) + (parts[5] + parts[7])
                fresh.append(old[m] - (even + odd))
            splat, ahead = fresh[:8], fresh[8:]
        inside = (lane >= 8 * g) & (lane < 8 * g + 8)
        panel = jnp.where(inside, -panel, panel)
        change = outer(before, panel)
        spread = [pick(panel, m) for m in range(8)]
        for r in range(16):
            if r == g:
                continue
            kept = jnp.where(inside, 0.0, rows[r])
            if r in near:
                parts = [near[r][m] * spread[m] for m in range(8)]
                even = (parts[0] + parts[2]) + (parts[4] + parts[6])
                odd = (parts[1] + parts[3]) + (parts[5] + parts[7])
                rows[r] = kept - (even + odd)
            else:
                rows[r] = kept - change[8 * r : 8 * r + 8, :]
        rows[g] = panel
        if later:
            later.pop(0)()
    while later:
        later.pop(0)()
    return jnp.concatenate(rows, axis=0)


def solve_kernel(shift_ratio, scale, samples, gram_ref, target_ref, cent_hbm, out_ref, cent, sems):
    blocks = samples // 128
    chunks = sems.shape[0]
    wide = cent.shape[1] // chunks

    def load(m):
        at = pl.ds(m * wide, wide)
        return pltpu.make_async_copy(cent_hbm.at[:, at], cent.at[:, at], sems.at[m])

    for m in range(chunks):
        load(m).start()
    eye = lax.broadcasted_iota(jnp.int32, (128, 128), 0) == lax.broadcasted_iota(jnp.int32, (128, 128), 1)
    base = [0]
    for k in range(blocks):
        base.append(base[-1] + samples - 128 * k)
    trace = jnp.zeros((1, 1), F32)
    for k in range(blocks):
        trace += jnp.sum(jnp.where(eye, gram_ref[base[k] : base[k] + 128, :], 0.0), axis=(0, 1), keepdims=True)
    shift = shift_ratio * trace / samples
    shift = jnp.where(eye, jnp.broadcast_to(shift, (128, 128)), 0.0)
    rhs = []
    tiles, quot = {}, {}
    for k in range(blocks):
        for i in range(k, blocks):
            at = base[k] + 128 * (i - k)
            tiles[i, k] = gram_ref[at : at + 128, :] + shift if i == k else gram_ref[at : at + 128, :]
        rhs.append(jnp.broadcast_to(target_ref[0:1, 128 * k : 128 * k + 128], (8, 128)))

    def divide(i, k, inv):
        def run():
            quot[i, k] = dot_nn(tiles[i, k], inv)

        return run

    def reduce(i, j, k):
        def run():
            tiles[i, j] = tiles[i, j] - dot_nt(quot[i, k], tiles[j, k])

        return run

    def lower(i, k, right):
        def run():
            rhs[i] = rhs[i] - dot_nt(right, quot[i, k])

        return run

    def close(k, right, inv):
        def run():
            rhs[k] = dot_nn(right, inv)

        return run

    later = []
    for k in range(blocks):
        inv = -sweep_block(tiles[k, k], later)
        later = []
        if k < blocks - 1:
            divide(k + 1, k, inv)()
            reduce(k + 1, k + 1, k)()
            later += [divide(i, k, inv) for i in range(k + 2, blocks)]
            later += [reduce(i, k + 1, k) for i in range(k + 2, blocks)]
            later += [reduce(i, j, k) for j in range(k + 2, blocks) for i in range(j, blocks)]
            later += [lower(i, k, rhs[k]) for i in range(k + 1, blocks)]
        if k < blocks - 1:
            later.append(close(k, rhs[k], inv))
        else:
            close(k, rhs[k], inv)()
    found = [None] * blocks
    for k in reversed(range(blocks)):
        x = rhs[k]
        for i in range(k + 1, blocks):
            x = x - dot_nn(found[i], quot[i, k])
        found[k] = x
    coeffs = jnp.concatenate(found, axis=1).astype(BF16)
    for m in range(chunks):
        load(m).wait()
        part = jnp.dot(coeffs, cent[:, m * wide : (m + 1) * wide], preferred_element_type=F32) * scale
        for i in range(wide // 128):
            r = m * wide // 128 + i
            out_ref[r : r + 1, :] = part[0:1, 128 * i : 128 * (i + 1)]


def solve(gram, target, centered):
    samples, width = centered.shape
    blocks = samples // 128
    vmem = pl.BlockSpec(memory_space=pltpu.VMEM)
    return pl.pallas_call(
        functools.partial(solve_kernel, SHIFT_RATIO, -math.sqrt(D * FF), samples),
        out_shape=jax.ShapeDtypeStruct((width // 128, 128), F32),
        in_specs=[vmem, vmem, pl.BlockSpec(memory_space=pl.ANY)],
        out_specs=vmem,
        scratch_shapes=[
            pltpu.VMEM((samples, width), BF16),
            pltpu.SemaphoreType.DMA((8,)),
        ],
        compiler_params=pltpu.CompilerParams(vmem_limit_bytes=60 << 20),
        name="solve",
    )(gram, target, centered)


LSIDE = 10
GROUP = 4
WIDE = 8 * 65


def enter(ids):
    barrier = pltpu.get_barrier_semaphore()
    for device in ids:
        pl.semaphore_signal(barrier, inc=1, device_id=device, device_id_type=MESH)
    pl.semaphore_wait(barrier, len(ids))


def remote(src, dst, send, recv, device):
    copy = pltpu.make_async_remote_copy(
        src_ref=src, dst_ref=dst, send_sem=send, recv_sem=recv, device_id=device, device_id_type=MESH
    )
    copy.start()
    return copy


def describe(src, dst, send, recv, device):
    return pltpu.make_async_remote_copy(
        src_ref=src, dst_ref=dst, send_sem=send, recv_sem=recv, device_id=device, device_id_type=MESH
    )


def each(first, last, body):
    def step(k, carry):
        body(k)
        return carry

    lax.fori_loop(first, last, step, 0)


def make_target(spins_ref, offdiag_ref, norm_scale):
    signs = (2 * spins_ref[...] - 1).astype(F32)
    sites = signs.shape[0]
    column = lax.rem(lax.broadcasted_iota(jnp.int32, signs.shape, 0), LSIDE)

    def turn(values, by):
        return jnp.concatenate([values[by:], values[:by]], axis=0)

    def next_column(values):
        return jnp.where(column == LSIDE - 1, turn(values, sites - LSIDE + 1), turn(values, 1))

    def last_column(values):
        return jnp.where(column == 0, turn(values, LSIDE - 1), turn(values, sites - 1))

    down = turn(signs, LSIDE)
    near = jnp.sum(signs * (next_column(signs) + down), axis=0, keepdims=True)
    distant = jnp.sum(signs * (next_column(down) + last_column(down)), axis=0, keepdims=True)
    energies = 0.25 * (near + SECOND_RATIO * distant) + offdiag_ref[...]
    return (energies - jnp.mean(energies, axis=1, keepdims=True)) * norm_scale


def main_kernel(
    stream_ref, win_ref, wout_ref, readout_ref, spins_ref, offdiag_ref, cent_out, gram_ref, target_ref,
    win, wout, hid, ht, hall, slope, acc, dsend, dl, dall, grad, cent, part_ref, twin, first, second,
    xs, xr, ws, wr, vs, vr, wws, wwr, vvs, vvr, sws, swr, svs, svr, hs, hr, ls, lr,
    sr, rr, sl, rl, fr, qr, fl, ql, bs, br, s0, r0, s1, r1, s2, r2, s3, r3, s4, r4, own, outs,
):
    s, p = lax.axis_index("samp"), lax.axis_index("par")
    x, c = s // 2, lax.rem(s, 2)
    y, z = p // 4, lax.rem(p, 4)
    sibling = s + 1 - 2 * c
    n = 16
    groups, tokens = 16, 25
    rows, dims, width, samples = 112, 64, 128, 512
    norm_scale = 1.0 / math.sqrt(samples)
    right, left, far = lax.rem(s + 2, 8), lax.rem(s + 6, 8), lax.rem(s + 4, 8)
    pars = [lax.rem(p + k, 16) for k in range(1, 16)]
    enter([(s, lax.rem(p + k, n)) for k in range(1, n)] + [(lax.rem(s + k, 8), p) for k in range(1, 8)])

    def at(a, b):
        return lax.rem(y + a, 4) * 4 + lax.rem(z + b, 4)

    def origin(a, b):
        return at(4 - a, 4 - b)

    def xcopy(k):
        return describe(win_ref, win.at[p, x, c], xs.at[k - 1], xr.at[k - 1], (lax.rem(s + 2 * k, 8), p))

    def w_first(k):
        return describe(win.at[p, :, c], win.at[p, :, c], ws.at[k - 1], wr.at[k - 1], (s, at(k, 0)))

    def w_then(a, m):
        q, i = origin(a, 0), 3 * a + m - 1
        return describe(win.at[q, :, c], win.at[q, :, c], wws.at[i], wwr.at[i], (s, at(0, m)))

    def v_first(k):
        return describe(wout.at[p, c], wout.at[p, c], vs.at[k - 1], vr.at[k - 1], (s, at(0, k)))

    def v_then(b, m):
        q, i = origin(0, b), 3 * b + m - 1
        return describe(wout.at[q, c], wout.at[q, c], vvs.at[i], vvr.at[i], (s, at(m, 0)))

    def w_across(i):
        q = origin(i // 4, lax.rem(i, 4))
        return describe(win.at[q, :, c], win.at[q, :, c], sws.at[i], swr.at[i], (sibling, p))

    def v_across(i):
        q = origin(i // 4, lax.rem(i, 4))
        return describe(wout.at[q, c], wout.at[q, c], svs.at[i], svr.at[i], (sibling, p))

    def hcopy(k, c):
        to, at_c, i = lax.rem(s + k, 8), pl.ds(pl.multiple_of(4 * c, 4), 4), 4 * (k - 1) + c
        return describe(ht.at[to, at_c], hall.at[s, at_c], hs.at[i], hr.at[i], (to, p))

    def lcopy(k):
        q = lax.rem(p + k, n)
        return describe(dsend.at[q], dl.at[p], ls.at[k - 1], lr.at[k - 1], (s, q))

    mine_w = pltpu.make_async_copy(win_ref, win.at[p, x, c], own.at[0])
    mine_v = pltpu.make_async_copy(wout_ref.at[pl.ds(pl.multiple_of(64 * c, 64), 64)], wout.at[p, c], own.at[1])
    mine_w.start()
    mine_v.start()
    each(1, 4, lambda k: xcopy(k).start())
    mine_v.wait()
    each(1, 4, lambda k: v_first(k).start())
    each(1, 4, lambda m: v_then(0, m).start())
    v_across(0).start()
    mine_w.wait()

    def prepare(four):
        for v in range(2):
            pair = 2 * four + v
            values = stream_ref[:, pl.ds(pl.multiple_of(8 * pair, 8), 8), :]
            mean = jnp.mean(values, axis=-1, keepdims=True)
            centered = values - mean
            variance = jnp.mean(centered * centered, axis=-1, keepdims=True)
            scaled = centered * lax.rsqrt(variance + EPSILON)
            for half in range(2):
                u = 2 * v + half
                g = 4 * four + u
                pieces = [jnp.zeros((4 * u, 512), F32)] if u > 0 else []
                pieces += [scaled[t, 4 * half : 4 * half + 4] for t in range(tokens)]
                pieces += [jnp.zeros((width - 4 * tokens - 4 * u, 512), F32)]
                hidden = jnp.concatenate(pieces, axis=0)

                @pl.when(g == p)
                def _(hidden=hidden):
                    hid[...] = hidden[:rows].astype(BF16)

                flipped = jnp.transpose(hidden).astype(BF16)
                for q in range(8):
                    ht[q, g] = flipped[64 * q : 64 * (q + 1), :]

    def open_w():
        each(1, 4, lambda k: xcopy(k).wait_recv())
        each(1, 4, lambda k: w_first(k).start())
        each(1, 4, lambda m: w_then(0, m).start())
        w_across(0).start()

    def pass_v(k):
        v_first(k).wait_recv()
        each(1, 4, lambda m: v_then(k, m).start())
        v_across(k).start()

    def pass_w(k):
        w_first(k).wait_recv()
        each(1, 4, lambda m: w_then(k, m).start())
        w_across(4 * k).start()

    def work(step):
        @pl.when(step == 1)
        def _():
            each(1, 4, pass_v)

        @pl.when(step == 2)
        def _():
            each(1, 4, pass_w)

        prepare(step)
        each(1, 8, lambda k: hcopy(k, step).start())

        @pl.when(step == 0)
        def _():
            open_w()

    each(0, 4, work)
    mine_h = pltpu.make_async_copy(ht.at[s], hall.at[s], own.at[2])
    mine_h.start()
    target_ref[...] = make_target(spins_ref, offdiag_ref, norm_scale)
    acc[...] = jnp.zeros_like(acc)

    def take(a):
        for b in range(4):
            if b > 0:
                w_then(a, b).wait_recv()
                w_across(4 * a + b).start()

            @pl.when(a > 0)
            def _():
                v_then(b, a).wait_recv()
                v_across(4 * a + b).start()

    def compute(a):
        row = lax.rem(y - a + 4, 4)
        for b in range(4):
            w_across(4 * a + b).wait_recv()
            v_across(4 * a + b).wait_recv()
        weights = jnp.concatenate([win[4 * row + j].reshape(512, 128) for j in range(4)], axis=1)
        preact = jnp.dot(hid[...], weights, preferred_element_type=F32)
        active, pull = jax.vjp(jax.nn.gelu, preact)
        slope[row] = pull(jnp.ones_like(preact))[0]
        acc[...] += jnp.dot(active.astype(BF16), wout[pl.ds(4 * row, 4)].reshape(512, 512), preferred_element_type=F32)

    take(0)

    def both(a):
        take(a)
        compute(a - 1)

    each(1, 4, both)
    compute(3)
    signal = (readout_ref[...] * jnp.tanh(acc[...])).astype(BF16)

    def back(i):
        row = lax.rem(y + jnp.where(i < 2, i, 5 - i), 4)
        weights = wout[pl.ds(4 * row, 4)].reshape(512, 512)
        backward = lax.dot_general(signal, weights, (((1,), (1,)), ((), ())), preferred_element_type=F32)
        delta = (backward * slope[row]).astype(BF16)
        for j in range(4):
            q = 4 * row + j
            dsend[q] = delta[:, 128 * j : 128 * (j + 1)]

            @pl.when(q != p)
            def _():
                lcopy(lax.rem(q - p + n, n)).start()

    each(0, 4, back)
    dl[p] = dsend[p]

    def chunk(i):
        return lax.rem(y + jnp.where(i == 0, 0, jnp.where(i == 1, 3, i - 1)), 4)

    def move(origin, i, send, recv, device):
        part = dall.at[origin, chunk(i)]
        return describe(part, part, send, recv, device)

    def to_right(i):
        return move(s, i, sr.at[i], rr.at[i], (right, p))

    def to_left(i):
        return move(s, i, sl.at[i], rl.at[i], (left, p))

    def on_right(j):
        return move(left, 2 * j, fr.at[j], qr.at[j], (right, p))

    def on_left(j):
        return move(right, 2 * j + 1, fl.at[j], ql.at[j], (left, p))

    def across(origin, i, slot):
        return move(origin, i, bs.at[slot + i], br.at[slot + i], (sibling, p))

    def begin(i):
        f = chunk(i)
        for j in range(4):
            q = 4 * f + j

            @pl.when(q != p)
            def _(q=q):
                lcopy(lax.rem(p - q + n, n)).wait_recv()

        for u in range(4):
            window = dl[4 * f + u]
            dall[s, f, 96 * u + 16 : 96 * u + 96, :] = window[16:96]
            if u == 0:
                dall[s, f, 0:16, :] = window[0:16]
            else:
                dall[s, f, 96 * u : 96 * u + 16, :] = window[0:16] + dl[4 * f + u - 1][96:112]
            if u == 3:
                dall[s, f, 384:400, :] = window[96:112]
        to_right(i).start()
        to_left(i).start()
        across(s, i, 0).start()

    each(0, 4, begin)
    mine_h.wait()

    lane = lax.broadcasted_iota(jnp.int32, (dims, width), 1)
    keep = [lax.rem(lane, GROUP) == i for i in range(GROUP)]
    fill = jnp.zeros((width - rows, 128), BF16)
    nothing = jnp.zeros((dims, width), BF16)

    def make(origin, i):
        f = chunk(i)
        for u in range(4):
            group = 4 * f + u
            flipped = hall[origin, group]
            delta = jnp.concatenate([dall[origin, f, 96 * u : 96 * u + rows, :], fill], axis=0)
            stack = jnp.concatenate([jnp.where(keep[v], flipped, nothing) for v in range(GROUP)], axis=0)
            grads = jnp.dot(stack, delta, preferred_element_type=F32).astype(BF16).astype(F32)
            for v in range(GROUP):
                grad[pl.ds(64 * origin + GROUP * group + v, dims, stride=WIDE), :] = grads[dims * v : dims * (v + 1), :]

    each(0, 4, lambda i: make(s, i))
    each(1, 8, lambda k: each(0, 4, lambda f: hcopy(k, f).wait_recv()))

    def near(i):
        to_right(i).wait_recv()
        to_left(i).wait_recv()

        @pl.when(lax.rem(i, 2) == 0)
        def _():
            on_right(i // 2).start()

        @pl.when(lax.rem(i, 2) == 1)
        def _():
            on_left(i // 2).start()

        across(left, i, 4).start()
        across(right, i, 8).start()
        make(left, i)
        make(right, i)

    each(0, 4, near)

    def beside(i):
        across(s, i, 0).wait_recv()
        make(sibling, i)

    each(0, 4, beside)

    def opposite(j):
        on_right(j).wait_recv()
        across(far, 2 * j, 12).start()
        on_left(j).wait_recv()
        across(far, 2 * j + 1, 12).start()
        make(far, 2 * j)
        make(far, 2 * j + 1)

    each(0, 2, opposite)

    def near_beside(i):
        across(left, i, 4).wait_recv()
        across(right, i, 8).wait_recv()
        make(sibling + left - s, i)
        make(sibling + right - s, i)

    each(0, 4, near_beside)

    def far_beside(i):
        across(far, i, 12).wait_recv()
        make(sibling + far - s, i)

    each(0, 4, far_beside)

    count = 4

    def center(m):
        for half in range(count):
            d = count * m + half
            values = grad[d * WIDE : d * WIDE + samples, :]
            mean = jnp.sum(values, axis=0, keepdims=True) * (1.0 / samples)
            cent[:, d * 128 : (d + 1) * 128] = ((values - mean) * norm_scale).astype(BF16)

    def store(m):
        at = pl.ds(m * 128 * count, 128 * count)
        return pltpu.make_async_copy(cent.at[:, at], cent_out.at[:, at], outs.at[m])

    def add(m):
        block = cent[:, m * 128 * count : (m + 1) * 128 * count]
        low = lax.dot_general(block, block[:256], (((1,), (1,)), ((), ())), preferred_element_type=F32)
        high = lax.dot_general(block[256:], block[256:], (((1,), (1,)), ((), ())), preferred_element_type=F32)
        for a, b, term in [(0, 512, low[:, :128]), (512, 896, low[128:, 128:]), (896, 1152, high[:, :128]), (1152, 1280, high[128:, 128:])]:
            if m == 0:
                part_ref[a:b, :] = term
            else:
                part_ref[a:b, :] += term

    steps = dims // count
    center(0)
    store(0).start()
    for m in range(1, steps):
        center(m)
        store(m).start()
        add(m - 1)
    add(steps - 1)

    core = c

    def slot(half, q):
        return pl.ds(pl.multiple_of(640 * half + 40 * q, 8), 40)

    give = pl.ds(pl.multiple_of(640 * (1 - core), 640), 640)
    keeps = pl.ds(pl.multiple_of(640 * core, 640), 640)
    copy = remote(part_ref.at[give], twin, s0.at[0], r0.at[0], (sibling, p))
    copy.wait_recv()
    part_ref[keeps, :] += twin[...]
    copies = [remote(part_ref.at[slot(core, q)], first.at[p], s1.at[k], r1.at[k], (s, q)) for k, q in enumerate(pars)]
    first[p] = part_ref[slot(core, p), :]
    for each_copy in copies:
        each_copy.wait_recv()
    total = first[0]
    for q in range(1, 16):
        total = total + first[q]
    second[x] = total
    more = [remote(second.at[x], second.at[x], s2.at[k], r2.at[k], (q, p)) for k, q in enumerate([right, far, left])]
    for each_copy in more:
        each_copy.wait_recv()
    total = second[0]
    for q in range(1, 4):
        total = total + second[q]
    gram_ref[slot(core, p), :] = total
    here = gram_ref.at[slot(core, p)]
    spread = [remote(here, here, s3.at[k], r3.at[k], (s, q)) for k, q in enumerate(pars)]
    passed = [remote(here, here, s4.at[15], r4.at[15], (sibling, p))]
    for k in range(15):
        spread[k].wait_recv()
        there = gram_ref.at[slot(core, lax.rem(p + 15 - k, 16))]
        passed.append(remote(there, there, s4.at[k], r4.at[k], (sibling, p)))
    for each_copy in passed:
        each_copy.wait()
    copy.wait_send()
    for each_copy in copies + more + spread:
        each_copy.wait_send()
    each(0, 4, lambda c: to_right(c).wait_send())
    each(0, 4, lambda c: to_left(c).wait_send())
    each(0, 2, lambda c: on_right(c).wait_send())
    each(0, 2, lambda c: on_left(c).wait_send())
    each(0, 4, lambda i: each(0, 4, lambda j: across(s, i, 4 * j).wait_send()))
    for m in range(steps):
        store(m).wait()
    each(1, n, lambda k: lcopy(k).wait_send())
    each(1, 8, lambda k: each(0, 4, lambda c: hcopy(k, c).wait_send()))
    each(1, 4, lambda k: xcopy(k).wait_send())
    each(1, 4, lambda k: w_first(k).wait_send())
    each(1, 4, lambda k: v_first(k).wait_send())
    each(0, 4, lambda k: each(1, 4, lambda m: w_then(k, m).wait_send()))
    each(0, 4, lambda k: each(1, 4, lambda m: v_then(k, m).wait_send()))
    each(0, n, lambda i: w_across(i).wait_send())
    each(0, n, lambda i: v_across(i).wait_send())


def make_gram(stream, weight_in, weight_out, readout, spins, offdiag):
    rows = 112
    sem = pltpu.SemaphoreType.DMA
    vmem = pl.BlockSpec(memory_space=pltpu.VMEM)
    counts = [3, 3, 3, 12, 12, 16, 16, 28, 15, 4, 4, 2, 2, 16, 1, 15, 3, 15, 16]
    return pl.pallas_call(
        main_kernel,
        out_shape=[
            jax.ShapeDtypeStruct((512, 8192), BF16),
            jax.ShapeDtypeStruct((1280, 128), F32),
            jax.ShapeDtypeStruct((1, 512), F32),
        ],
        in_specs=[vmem] * 6,
        out_specs=[pl.BlockSpec(memory_space=pl.ANY), vmem, vmem],
        scratch_shapes=[
            pltpu.VMEM((16, 4, 2, 64, 128), BF16),
            pltpu.VMEM((16, 2, 64, 512), BF16),
            pltpu.VMEM((rows, 512), BF16),
            pltpu.VMEM((8, 16, 64, 128), BF16),
            pltpu.VMEM((8, 16, 64, 128), BF16),
            pltpu.VMEM((4, rows, 512), F32),
            pltpu.VMEM((rows, 512), F32),
            pltpu.VMEM((16, rows, 128), BF16),
            pltpu.VMEM((16, rows, 128), BF16),
            pltpu.VMEM((8, 4, 400, 128), BF16),
            pltpu.VMEM((65 * WIDE, 128), F32),
            pltpu.VMEM((512, 8192), BF16),
            pltpu.VMEM((1280, 128), F32),
            pltpu.VMEM((640, 128), F32),
            pltpu.VMEM((16, 40, 128), F32),
            pltpu.VMEM((4, 40, 128), F32),
        ]
        + [sem((count,)) for count in counts for _ in range(2)]
        + [sem((3,)), sem((16,))],
        compiler_params=pltpu.CompilerParams(collective_id=1, has_side_effects=True, vmem_limit_bytes=60 << 20),
        name="make_gram",
    )(stream, weight_in, weight_out, readout, spins, offdiag)


def per_device(stream, weight_in, weight_out, readout, spins, offdiag):
    centered, gram, target = make_gram(
        jnp.transpose(stream, (1, 0, 2)), weight_in, weight_out, readout[None, :], jnp.transpose(spins), offdiag[None, :]
    )
    return solve(gram, target, centered)


def solution(mesh):
    return jax.shard_map(
        per_device,
        mesh=mesh,
        in_specs=(P("samp", None, None), P("samp", "par"), P("par", None), P(), P(), P()),
        out_specs=P("samp", "par"),
        check_vma=False,
    )
```

```python
import functools
import math

import jax
import jax.numpy as jnp
from jax import lax
from jax.experimental import pallas as pl
from jax.experimental.pallas import tpu as pltpu
from jax.sharding import PartitionSpec as P

D = 512
FF = 2048
EPSILON = 1e-05
SHIFT_RATIO = 0.1
SECOND_RATIO = 0.5
MESH = pl.DeviceIdType.MESH
F32 = jnp.float32
BF16 = jnp.bfloat16
HI = lax.Precision.HIGHEST


def dot_nn(a, b):
    return lax.dot_general(a, b, (((1,), (0,)), ((), ())), precision=HI, preferred_element_type=F32)


def dot_nt(a, b):
    return lax.dot_general(a, b, (((1,), (1,)), ((), ())), precision=HI, preferred_element_type=F32)


def thirds(values):
    high = values.astype(BF16).astype(F32)
    rest = values - high
    middle = rest.astype(BF16).astype(F32)
    return high, middle, rest - middle


def outer(left, right):
    a, b, c = thirds(left)
    d, e, f = thirds(right)
    lhs = jnp.concatenate([a, a, b, a, b, c], axis=0).astype(BF16)
    rhs = jnp.concatenate([d, e, d, f, e, d], axis=0).astype(BF16)
    return lax.dot_general(lhs, rhs, (((0,), (0,)), ((), ())), preferred_element_type=F32)


def spread_column(values, at):
    return jnp.broadcast_to(values[:, at : at + 1], (8, 128))


def pick(values, row):
    return jnp.broadcast_to(values[row : row + 1, :], (8, 128))


def sweep_block(block, later):
    lane = lax.broadcasted_iota(jnp.int32, (8, 128), 1)
    sub = lax.broadcasted_iota(jnp.int32, (8, 128), 0)
    units = [jnp.where(sub == i, 1.0, 0.0) for i in range(8)]
    rows = [block[8 * r : 8 * r + 8, :] for r in range(16)]
    splat = [spread_column(rows[0], m) for m in range(8)]
    ahead = [spread_column(rows[0], 8 + m) for m in range(8)]
    for g in range(16):
        panel = rows[g]
        before = panel
        last = g == 15
        beyond = [spread_column(panel, 8 * g + 16 + m) for m in range(8)] if g < 14 else []
        old = [] if last else [spread_column(rows[g + 1], 8 * g + 8 + m) for m in range(16 if g < 14 else 8)]
        near = {r: [spread_column(rows[r], 8 * g + m) for m in range(8)] for r in (g + 1, g + 2) if r < 16}
        for i in range(8):
            factor = (splat[i] - units[i]) * (1.0 / pick(splat[i], i))
            panel = jnp.where(lane == 8 * g + i, units[i], panel)
            panel = panel - factor * pick(panel, i)
            for m in range(i + 1, 8):
                splat[m] = splat[m] - factor * pick(splat[m], i)
            ahead = [values - factor * pick(values, i) for values in ahead]
            beyond = [values - factor * pick(values, i) for values in beyond]
        if not last:
            fresh = []
            for m, values in enumerate(ahead + beyond):
                parts = [near[g + 1][j] * pick(values, j) for j in range(8)]
                even = (parts[0] + parts[2]) + (parts[4] + parts[6])
                odd = (parts[1] + parts[3]) + (parts[5] + parts[7])
                fresh.append(old[m] - (even + odd))
            splat, ahead = fresh[:8], fresh[8:]
        inside = (lane >= 8 * g) & (lane < 8 * g + 8)
        panel = jnp.where(inside, -panel, panel)
        change = outer(before, panel)
        spread = [pick(panel, m) for m in range(8)]
        for r in range(16):
            if r == g:
                continue
            kept = jnp.where(inside, 0.0, rows[r])
            if r in near:
                parts = [near[r][m] * spread[m] for m in range(8)]
                even = (parts[0] + parts[2]) + (parts[4] + parts[6])
                odd = (parts[1] + parts[3]) + (parts[5] + parts[7])
                rows[r] = kept - (even + odd)
            else:
                rows[r] = kept - change[8 * r : 8 * r + 8, :]
        rows[g] = panel
        if later:
            later.pop(0)()
    while later:
        later.pop(0)()
    return jnp.concatenate(rows, axis=0)


def solve_kernel(shift_ratio, scale, samples, gram_ref, target_ref, cent_hbm, out_ref, cent, sems):
    blocks = samples // 128
    chunks = sems.shape[0]
    wide = cent.shape[1] // chunks

    def load(m):
        at = pl.ds(m * wide, wide)
        return pltpu.make_async_copy(cent_hbm.at[:, at], cent.at[:, at], sems.at[m])

    for m in range(chunks):
        load(m).start()
    eye = lax.broadcasted_iota(jnp.int32, (128, 128), 0) == lax.broadcasted_iota(jnp.int32, (128, 128), 1)
    base = [0]
    for k in range(blocks):
        base.append(base[-1] + samples - 128 * k)
    trace = jnp.zeros((1, 1), F32)
    for k in range(blocks):
        trace += jnp.sum(jnp.where(eye, gram_ref[base[k] : base[k] + 128, :], 0.0), axis=(0, 1), keepdims=True)
    shift = shift_ratio * trace / samples
    shift = jnp.where(eye, jnp.broadcast_to(shift, (128, 128)), 0.0)
    rhs = []
    tiles, quot = {}, {}
    for k in range(blocks):
        for i in range(k, blocks):
            at = base[k] + 128 * (i - k)
            tiles[i, k] = gram_ref[at : at + 128, :] + shift if i == k else gram_ref[at : at + 128, :]
        rhs.append(jnp.broadcast_to(target_ref[0:1, 128 * k : 128 * k + 128], (8, 128)))

    def divide(i, k, inv):
        def run():
            quot[i, k] = dot_nn(tiles[i, k], inv)

        return run

    def reduce(i, j, k):
        def run():
            tiles[i, j] = tiles[i, j] - dot_nt(quot[i, k], tiles[j, k])

        return run

    def lower(i, k, right):
        def run():
            rhs[i] = rhs[i] - dot_nt(right, quot[i, k])

        return run

    def close(k, right, inv):
        def run():
            rhs[k] = dot_nn(right, inv)

        return run

    later = []
    for k in range(blocks):
        inv = -sweep_block(tiles[k, k], later)
        later = []
        if k < blocks - 1:
            divide(k + 1, k, inv)()
            reduce(k + 1, k + 1, k)()
            later += [divide(i, k, inv) for i in range(k + 2, blocks)]
            later += [reduce(i, k + 1, k) for i in range(k + 2, blocks)]
            later += [reduce(i, j, k) for j in range(k + 2, blocks) for i in range(j, blocks)]
            later += [lower(i, k, rhs[k]) for i in range(k + 1, blocks)]
        if k < blocks - 1:
            later.append(close(k, rhs[k], inv))
        else:
            close(k, rhs[k], inv)()
    found = [None] * blocks
    for k in reversed(range(blocks)):
        x = rhs[k]
        for i in range(k + 1, blocks):
            x = x - dot_nn(found[i], quot[i, k])
        found[k] = x
    coeffs = jnp.concatenate(found, axis=1).astype(BF16)
    for m in range(chunks):
        load(m).wait()
        part = jnp.dot(coeffs, cent[:, m * wide : (m + 1) * wide], preferred_element_type=F32) * scale
        for i in range(wide // 128):
            r = m * wide // 128 + i
            out_ref[r : r + 1, :] = part[0:1, 128 * i : 128 * (i + 1)]


def solve(gram, target, centered):
    samples, width = centered.shape
    blocks = samples // 128
    vmem = pl.BlockSpec(memory_space=pltpu.VMEM)
    return pl.pallas_call(
        functools.partial(solve_kernel, SHIFT_RATIO, -math.sqrt(D * FF), samples),
        out_shape=jax.ShapeDtypeStruct((width // 128, 128), F32),
        in_specs=[vmem, vmem, pl.BlockSpec(memory_space=pl.ANY)],
        out_specs=vmem,
        scratch_shapes=[
            pltpu.VMEM((samples, width), BF16),
            pltpu.SemaphoreType.DMA((8,)),
        ],
        compiler_params=pltpu.CompilerParams(vmem_limit_bytes=60 << 20),
        name="solve",
    )(gram, target, centered)


LSIDE = 10
GROUP = 4
WIDE = 8 * 65


def enter(ids):
    barrier = pltpu.get_barrier_semaphore()
    for device in ids:
        pl.semaphore_signal(barrier, inc=1, device_id=device, device_id_type=MESH)
    pl.semaphore_wait(barrier, len(ids))


def remote(src, dst, send, recv, device):
    copy = pltpu.make_async_remote_copy(
        src_ref=src, dst_ref=dst, send_sem=send, recv_sem=recv, device_id=device, device_id_type=MESH
    )
    copy.start()
    return copy


def describe(src, dst, send, recv, device):
    return pltpu.make_async_remote_copy(
        src_ref=src, dst_ref=dst, send_sem=send, recv_sem=recv, device_id=device, device_id_type=MESH
    )


def each(first, last, body):
    def step(k, carry):
        body(k)
        return carry

    lax.fori_loop(first, last, step, 0)


def make_target(spins_ref, offdiag_ref, norm_scale):
    signs = (2 * spins_ref[...] - 1).astype(F32)
    sites = signs.shape[0]
    column = lax.rem(lax.broadcasted_iota(jnp.int32, signs.shape, 0), LSIDE)

    def turn(values, by):
        return jnp.concatenate([values[by:], values[:by]], axis=0)

    def next_column(values):
        return jnp.where(column == LSIDE - 1, turn(values, sites - LSIDE + 1), turn(values, 1))

    def last_column(values):
        return jnp.where(column == 0, turn(values, LSIDE - 1), turn(values, sites - 1))

    down = turn(signs, LSIDE)
    near = jnp.sum(signs * (next_column(signs) + down), axis=0, keepdims=True)
    distant = jnp.sum(signs * (next_column(down) + last_column(down)), axis=0, keepdims=True)
    energies = 0.25 * (near + SECOND_RATIO * distant) + offdiag_ref[...]
    return (energies - jnp.mean(energies, axis=1, keepdims=True)) * norm_scale


def main_kernel(
    stream_hbm, win_ref, wout_ref, readout_ref, spins_ref, offdiag_ref, cent_out, gram_ref, target_ref, stream_ref,
    win, wout, hid, ht, hall, slope, acc, dsend, dl, dall, grad, cent, part_ref, twin, first, second,
    xs, xr, ws, wr, vs, vr, wws, wwr, vvs, vvr, sws, swr, svs, svr, hs, hr, ls, lr,
    sr, rr, sl, rl, fr, qr, fl, ql, bs, br, s0, r0, s1, r1, s2, r2, s3, r3, s4, r4, own, outs,
):
    s, p = lax.axis_index("samp"), lax.axis_index("par")
    x, c = s // 2, lax.rem(s, 2)
    y, z = p // 4, lax.rem(p, 4)
    sibling = s + 1 - 2 * c
    n = 16
    groups, tokens = 16, 25
    fetch = pltpu.make_async_copy(stream_hbm, stream_ref, own.at[3])
    fetch.start()
    rows, dims, width, samples = 112, 64, 128, 512
    norm_scale = 1.0 / math.sqrt(samples)
    right, left, far = lax.rem(s + 2, 8), lax.rem(s + 6, 8), lax.rem(s + 4, 8)
    pars = [lax.rem(p + k, 16) for k in range(1, 16)]
    enter([(s, lax.rem(p + k, n)) for k in range(1, n)] + [(lax.rem(s + k, 8), p) for k in range(1, 8)])

    def at(a, b):
        return lax.rem(y + a, 4) * 4 + lax.rem(z + b, 4)

    def origin(a, b):
        return at(4 - a, 4 - b)

    def xcopy(k):
        return describe(win_ref, win.at[p, x, c], xs.at[k - 1], xr.at[k - 1], (lax.rem(s + 2 * k, 8), p))

    def w_first(k):
        return describe(win.at[p, :, c], win.at[p, :, c], ws.at[k - 1], wr.at[k - 1], (s, at(k, 0)))

    def w_then(a, m):
        q, i = origin(a, 0), 3 * a + m - 1
        return describe(win.at[q, :, c], win.at[q, :, c], wws.at[i], wwr.at[i], (s, at(0, m)))

    def v_first(k):
        return describe(wout.at[p, c], wout.at[p, c], vs.at[k - 1], vr.at[k - 1], (s, at(0, k)))

    def v_then(b, m):
        q, i = origin(0, b), 3 * b + m - 1
        return describe(wout.at[q, c], wout.at[q, c], vvs.at[i], vvr.at[i], (s, at(m, 0)))

    def w_across(i):
        q = origin(i // 4, lax.rem(i, 4))
        return describe(win.at[q, :, c], win.at[q, :, c], sws.at[i], swr.at[i], (sibling, p))

    def v_across(i):
        q = origin(i // 4, lax.rem(i, 4))
        return describe(wout.at[q, c], wout.at[q, c], svs.at[i], svr.at[i], (sibling, p))

    def hcopy(k, c):
        to, at_c, i = lax.rem(s + k, 8), pl.ds(pl.multiple_of(4 * c, 4), 4), 4 * (k - 1) + c
        return describe(ht.at[to, at_c], hall.at[s, at_c], hs.at[i], hr.at[i], (to, p))

    def lcopy(k):
        q = lax.rem(p + k, n)
        return describe(dsend.at[q], dl.at[p], ls.at[k - 1], lr.at[k - 1], (s, q))

    mine_w = pltpu.make_async_copy(win_ref, win.at[p, x, c], own.at[0])
    mine_v = pltpu.make_async_copy(wout_ref.at[pl.ds(pl.multiple_of(64 * c, 64), 64)], wout.at[p, c], own.at[1])
    mine_w.start()
    mine_v.start()
    each(1, 4, lambda k: xcopy(k).start())
    mine_v.wait()
    each(1, 4, lambda k: v_first(k).start())
    each(1, 4, lambda m: v_then(0, m).start())
    v_across(0).start()
    mine_w.wait()

    def prepare(four):
        for v in range(2):
            pair = 2 * four + v
            values = stream_ref[:, pl.ds(pl.multiple_of(8 * pair, 8), 8), :]
            mean = jnp.mean(values, axis=-1, keepdims=True)
            centered = values - mean
            variance = jnp.mean(centered * centered, axis=-1, keepdims=True)
            scaled = centered * lax.rsqrt(variance + EPSILON)
            for half in range(2):
                u = 2 * v + half
                g = 4 * four + u
                pieces = [jnp.zeros((4 * u, 512), F32)] if u > 0 else []
                pieces += [scaled[t, 4 * half : 4 * half + 4] for t in range(tokens)]
                pieces += [jnp.zeros((width - 4 * tokens - 4 * u, 512), F32)]
                hidden = jnp.concatenate(pieces, axis=0)

                @pl.when(g == p)
                def _(hidden=hidden):
                    hid[...] = hidden[:rows].astype(BF16)

                flipped = jnp.transpose(hidden).astype(BF16)
                for q in range(8):
                    ht[q, g] = flipped[64 * q : 64 * (q + 1), :]

    def open_w():
        each(1, 4, lambda k: xcopy(k).wait_recv())
        each(1, 4, lambda k: w_first(k).start())
        each(1, 4, lambda m: w_then(0, m).start())
        w_across(0).start()

    def pass_v(k):
        v_first(k).wait_recv()
        each(1, 4, lambda m: v_then(k, m).start())
        v_across(k).start()

    def pass_w(k):
        w_first(k).wait_recv()
        each(1, 4, lambda m: w_then(k, m).start())
        w_across(4 * k).start()

    def work(step):
        @pl.when(step == 1)
        def _():
            each(1, 4, pass_v)

        @pl.when(step == 2)
        def _():
            each(1, 4, pass_w)

        prepare(step)
        each(1, 8, lambda k: hcopy(k, step).start())

        @pl.when(step == 0)
        def _():
            open_w()

    fetch.wait()
    each(0, 4, work)
    mine_h = pltpu.make_async_copy(ht.at[s], hall.at[s], own.at[2])
    mine_h.start()
    target_ref[...] = make_target(spins_ref, offdiag_ref, norm_scale)
    acc[...] = jnp.zeros_like(acc)

    def take(a):
        for b in range(4):
            if b > 0:
                w_then(a, b).wait_recv()
                w_across(4 * a + b).start()

            @pl.when(a > 0)
            def _():
                v_then(b, a).wait_recv()
                v_across(4 * a + b).start()

    def compute(a):
        row = lax.rem(y - a + 4, 4)
        for b in range(4):
            w_across(4 * a + b).wait_recv()
            v_across(4 * a + b).wait_recv()
        weights = jnp.concatenate([win[4 * row + j].reshape(512, 128) for j in range(4)], axis=1)
        preact = jnp.dot(hid[...], weights, preferred_element_type=F32)
        active, pull = jax.vjp(jax.nn.gelu, preact)
        slope[row] = pull(jnp.ones_like(preact))[0]
        acc[...] += jnp.dot(active.astype(BF16), wout[pl.ds(4 * row, 4)].reshape(512, 512), preferred_element_type=F32)

    take(0)

    def both(a):
        take(a)
        compute(a - 1)

    each(1, 4, both)
    compute(3)
    signal = (readout_ref[...] * jnp.tanh(acc[...])).astype(BF16)

    def back(i):
        row = lax.rem(y + jnp.where(i < 2, i, 5 - i), 4)
        weights = wout[pl.ds(4 * row, 4)].reshape(512, 512)
        backward = lax.dot_general(signal, weights, (((1,), (1,)), ((), ())), preferred_element_type=F32)
        delta = (backward * slope[row]).astype(BF16)
        for j in range(4):
            q = 4 * row + j
            dsend[q] = delta[:, 128 * j : 128 * (j + 1)]

            @pl.when(q != p)
            def _():
                lcopy(lax.rem(q - p + n, n)).start()

    each(0, 4, back)
    dl[p] = dsend[p]

    def chunk(i):
        return lax.rem(y + jnp.where(i == 0, 0, jnp.where(i == 1, 3, i - 1)), 4)

    def move(origin, i, send, recv, device):
        part = dall.at[origin, chunk(i)]
        return describe(part, part, send, recv, device)

    def to_right(i):
        return move(s, i, sr.at[i], rr.at[i], (right, p))

    def to_left(i):
        return move(s, i, sl.at[i], rl.at[i], (left, p))

    def on_right(j):
        return move(left, 2 * j, fr.at[j], qr.at[j], (right, p))

    def on_left(j):
        return move(right, 2 * j + 1, fl.at[j], ql.at[j], (left, p))

    def across(origin, i, slot):
        return move(origin, i, bs.at[slot + i], br.at[slot + i], (sibling, p))

    def begin(i):
        f = chunk(i)
        for j in range(4):
            q = 4 * f + j

            @pl.when(q != p)
            def _(q=q):
                lcopy(lax.rem(p - q + n, n)).wait_recv()

        for u in range(4):
            window = dl[4 * f + u]
            dall[s, f, 96 * u + 16 : 96 * u + 96, :] = window[16:96]
            if u == 0:
                dall[s, f, 0:16, :] = window[0:16]
            else:
                dall[s, f, 96 * u : 96 * u + 16, :] = window[0:16] + dl[4 * f + u - 1][96:112]
            if u == 3:
                dall[s, f, 384:400, :] = window[96:112]
        to_right(i).start()
        to_left(i).start()
        across(s, i, 0).start()

    each(0, 4, begin)
    mine_h.wait()

    lane = lax.broadcasted_iota(jnp.int32, (dims, width), 1)
    keep = [lax.rem(lane, GROUP) == i for i in range(GROUP)]
    fill = jnp.zeros((width - rows, 128), BF16)
    nothing = jnp.zeros((dims, width), BF16)

    def make(origin, i):
        f = chunk(i)
        for u in range(4):
            group = 4 * f + u
            flipped = hall[origin, group]
            delta = jnp.concatenate([dall[origin, f, 96 * u : 96 * u + rows, :], fill], axis=0)
            stack = jnp.concatenate([jnp.where(keep[v], flipped, nothing) for v in range(GROUP)], axis=0)
            grads = jnp.dot(stack, delta, preferred_element_type=F32).astype(BF16).astype(F32)
            for v in range(GROUP):
                grad[pl.ds(64 * origin + GROUP * group + v, dims, stride=WIDE), :] = grads[dims * v : dims * (v + 1), :]

    each(0, 4, lambda i: make(s, i))
    each(1, 8, lambda k: each(0, 4, lambda f: hcopy(k, f).wait_recv()))

    def near(i):
        to_right(i).wait_recv()
        to_left(i).wait_recv()

        @pl.when(lax.rem(i, 2) == 0)
        def _():
            on_right(i // 2).start()

        @pl.when(lax.rem(i, 2) == 1)
        def _():
            on_left(i // 2).start()

        across(left, i, 4).start()
        across(right, i, 8).start()
        make(left, i)
        make(right, i)

    each(0, 4, near)

    def beside(i):
        across(s, i, 0).wait_recv()
        make(sibling, i)

    each(0, 4, beside)

    def opposite(j):
        on_right(j).wait_recv()
        across(far, 2 * j, 12).start()
        on_left(j).wait_recv()
        across(far, 2 * j + 1, 12).start()
        make(far, 2 * j)
        make(far, 2 * j + 1)

    each(0, 2, opposite)

    def near_beside(i):
        across(left, i, 4).wait_recv()
        across(right, i, 8).wait_recv()
        make(sibling + left - s, i)
        make(sibling + right - s, i)

    each(0, 4, near_beside)

    def far_beside(i):
        across(far, i, 12).wait_recv()
        make(sibling + far - s, i)

    each(0, 4, far_beside)

    count = 4

    def center(m):
        for half in range(count):
            d = count * m + half
            values = grad[d * WIDE : d * WIDE + samples, :]
            mean = jnp.sum(values, axis=0, keepdims=True) * (1.0 / samples)
            cent[:, d * 128 : (d + 1) * 128] = ((values - mean) * norm_scale).astype(BF16)

    def store(m):
        at = pl.ds(m * 128 * count, 128 * count)
        return pltpu.make_async_copy(cent.at[:, at], cent_out.at[:, at], outs.at[m])

    def add(m):
        block = cent[:, m * 128 * count : (m + 1) * 128 * count]
        low = lax.dot_general(block, block[:256], (((1,), (1,)), ((), ())), preferred_element_type=F32)
        high = lax.dot_general(block[256:], block[256:], (((1,), (1,)), ((), ())), preferred_element_type=F32)
        for a, b, term in [(0, 512, low[:, :128]), (512, 896, low[128:, 128:]), (896, 1152, high[:, :128]), (1152, 1280, high[128:, 128:])]:
            if m == 0:
                part_ref[a:b, :] = term
            else:
                part_ref[a:b, :] += term

    steps = dims // count
    center(0)
    store(0).start()
    for m in range(1, steps):
        center(m)
        store(m).start()
        add(m - 1)
    add(steps - 1)

    core = c

    def slot(half, q):
        return pl.ds(pl.multiple_of(640 * half + 40 * q, 8), 40)

    give = pl.ds(pl.multiple_of(640 * (1 - core), 640), 640)
    keeps = pl.ds(pl.multiple_of(640 * core, 640), 640)
    copy = remote(part_ref.at[give], twin, s0.at[0], r0.at[0], (sibling, p))
    copy.wait_recv()
    part_ref[keeps, :] += twin[...]
    copies = [remote(part_ref.at[slot(core, q)], first.at[p], s1.at[k], r1.at[k], (s, q)) for k, q in enumerate(pars)]
    first[p] = part_ref[slot(core, p), :]
    for each_copy in copies:
        each_copy.wait_recv()
    total = first[0]
    for q in range(1, 16):
        total = total + first[q]
    second[x] = total
    more = [remote(second.at[x], second.at[x], s2.at[k], r2.at[k], (q, p)) for k, q in enumerate([right, far, left])]
    for each_copy in more:
        each_copy.wait_recv()
    total = second[0]
    for q in range(1, 4):
        total = total + second[q]
    gram_ref[slot(core, p), :] = total
    here = gram_ref.at[slot(core, p)]
    spread = [remote(here, here, s3.at[k], r3.at[k], (s, q)) for k, q in enumerate(pars)]
    passed = [remote(here, here, s4.at[15], r4.at[15], (sibling, p))]
    for k in range(15):
        spread[k].wait_recv()
        there = gram_ref.at[slot(core, lax.rem(p + 15 - k, 16))]
        passed.append(remote(there, there, s4.at[k], r4.at[k], (sibling, p)))
    for each_copy in passed:
        each_copy.wait()
    copy.wait_send()
    for each_copy in copies + more + spread:
        each_copy.wait_send()
    each(0, 4, lambda c: to_right(c).wait_send())
    each(0, 4, lambda c: to_left(c).wait_send())
    each(0, 2, lambda c: on_right(c).wait_send())
    each(0, 2, lambda c: on_left(c).wait_send())
    each(0, 4, lambda i: each(0, 4, lambda j: across(s, i, 4 * j).wait_send()))
    for m in range(steps):
        store(m).wait()
    each(1, n, lambda k: lcopy(k).wait_send())
    each(1, 8, lambda k: each(0, 4, lambda c: hcopy(k, c).wait_send()))
    each(1, 4, lambda k: xcopy(k).wait_send())
    each(1, 4, lambda k: w_first(k).wait_send())
    each(1, 4, lambda k: v_first(k).wait_send())
    each(0, 4, lambda k: each(1, 4, lambda m: w_then(k, m).wait_send()))
    each(0, 4, lambda k: each(1, 4, lambda m: v_then(k, m).wait_send()))
    each(0, n, lambda i: w_across(i).wait_send())
    each(0, n, lambda i: v_across(i).wait_send())


def make_gram(stream, weight_in, weight_out, readout, spins, offdiag):
    rows = 112
    sem = pltpu.SemaphoreType.DMA
    vmem = pl.BlockSpec(memory_space=pltpu.VMEM)
    counts = [3, 3, 3, 12, 12, 16, 16, 28, 15, 4, 4, 2, 2, 16, 1, 15, 3, 15, 16]
    return pl.pallas_call(
        main_kernel,
        out_shape=[
            jax.ShapeDtypeStruct((512, 8192), BF16),
            jax.ShapeDtypeStruct((1280, 128), F32),
            jax.ShapeDtypeStruct((1, 512), F32),
        ],
        in_specs=[pl.BlockSpec(memory_space=pl.ANY)] * 3 + [vmem] * 3,
        out_specs=[pl.BlockSpec(memory_space=pl.ANY), vmem, vmem],
        scratch_shapes=[
            pltpu.VMEM((25, 64, 512), F32),
            pltpu.VMEM((16, 4, 2, 64, 128), BF16),
            pltpu.VMEM((16, 2, 64, 512), BF16),
            pltpu.VMEM((rows, 512), BF16),
            pltpu.VMEM((8, 16, 64, 128), BF16),
            pltpu.VMEM((8, 16, 64, 128), BF16),
            pltpu.VMEM((4, rows, 512), F32),
            pltpu.VMEM((rows, 512), F32),
            pltpu.VMEM((16, rows, 128), BF16),
            pltpu.VMEM((16, rows, 128), BF16),
            pltpu.VMEM((8, 4, 400, 128), BF16),
            pltpu.VMEM((65 * WIDE, 128), F32),
            pltpu.VMEM((512, 8192), BF16),
            pltpu.VMEM((1280, 128), F32),
            pltpu.VMEM((640, 128), F32),
            pltpu.VMEM((16, 40, 128), F32),
            pltpu.VMEM((4, 40, 128), F32),
        ]
        + [sem((count,)) for count in counts for _ in range(2)]
        + [sem((4,)), sem((16,))],
        compiler_params=pltpu.CompilerParams(collective_id=1, has_side_effects=True, vmem_limit_bytes=60 << 20),
        name="make_gram",
    )(stream, weight_in, weight_out, readout, spins, offdiag)


def per_device(stream, weight_in, weight_out, readout, spins, offdiag):
    centered, gram, target = make_gram(
        jnp.transpose(stream, (1, 0, 2)), weight_in, weight_out, readout[None, :], jnp.transpose(spins), offdiag[None, :]
    )
    return solve(gram, target, centered)


def solution(mesh):
    return jax.shard_map(
        per_device,
        mesh=mesh,
        in_specs=(P("samp", None, None), P("samp", "par"), P("par", None), P(), P(), P()),
        out_specs=P("samp", "par"),
        check_vma=False,
    )
```

```python
import functools
import math

import jax
import jax.numpy as jnp
from jax import lax
from jax.experimental import pallas as pl
from jax.experimental.pallas import tpu as pltpu
from jax.sharding import PartitionSpec as P

D = 512
FF = 2048
EPSILON = 1e-05
SHIFT_RATIO = 0.1
SECOND_RATIO = 0.5
MESH = pl.DeviceIdType.MESH
F32 = jnp.float32
BF16 = jnp.bfloat16
HI = lax.Precision.HIGHEST


def dot_nn(a, b):
    return lax.dot_general(a, b, (((1,), (0,)), ((), ())), precision=HI, preferred_element_type=F32)


def dot_nt(a, b):
    return lax.dot_general(a, b, (((1,), (1,)), ((), ())), precision=HI, preferred_element_type=F32)


def thirds(values):
    high = values.astype(BF16).astype(F32)
    rest = values - high
    middle = rest.astype(BF16).astype(F32)
    return high, middle, rest - middle


def outer(left, right):
    a, b, c = thirds(left)
    d, e, f = thirds(right)
    lhs = jnp.concatenate([a, a, b, a, b, c], axis=0).astype(BF16)
    rhs = jnp.concatenate([d, e, d, f, e, d], axis=0).astype(BF16)
    return lax.dot_general(lhs, rhs, (((0,), (0,)), ((), ())), preferred_element_type=F32)


def spread_column(values, at):
    return jnp.broadcast_to(values[:, at : at + 1], (8, 128))


def pick(values, row):
    return jnp.broadcast_to(values[row : row + 1, :], (8, 128))


def sweep_block(block, later):
    lane = lax.broadcasted_iota(jnp.int32, (8, 128), 1)
    sub = lax.broadcasted_iota(jnp.int32, (8, 128), 0)
    units = [jnp.where(sub == i, 1.0, 0.0) for i in range(8)]
    rows = [block[8 * r : 8 * r + 8, :] for r in range(16)]
    splat = [spread_column(rows[0], m) for m in range(8)]
    ahead = [spread_column(rows[0], 8 + m) for m in range(8)]
    for g in range(16):
        panel = rows[g]
        before = panel
        last = g == 15
        beyond = [spread_column(panel, 8 * g + 16 + m) for m in range(8)] if g < 14 else []
        old = [] if last else [spread_column(rows[g + 1], 8 * g + 8 + m) for m in range(16 if g < 14 else 8)]
        near = {r: [spread_column(rows[r], 8 * g + m) for m in range(8)] for r in (g + 1, g + 2) if r < 16}
        for i in range(8):
            factor = (splat[i] - units[i]) * (1.0 / pick(splat[i], i))
            panel = jnp.where(lane == 8 * g + i, units[i], panel)
            panel = panel - factor * pick(panel, i)
            for m in range(i + 1, 8):
                splat[m] = splat[m] - factor * pick(splat[m], i)
            ahead = [values - factor * pick(values, i) for values in ahead]
            beyond = [values - factor * pick(values, i) for values in beyond]
        if not last:
            fresh = []
            for m, values in enumerate(ahead + beyond):
                parts = [near[g + 1][j] * pick(values, j) for j in range(8)]
                even = (parts[0] + parts[2]) + (parts[4] + parts[6])
                odd = (parts[1] + parts[3]) + (parts[5] + parts[7])
                fresh.append(old[m] - (even + odd))
            splat, ahead = fresh[:8], fresh[8:]
        inside = (lane >= 8 * g) & (lane < 8 * g + 8)
        panel = jnp.where(inside, -panel, panel)
        change = outer(before, panel)
        spread = [pick(panel, m) for m in range(8)]
        for r in range(16):
            if r == g:
                continue
            kept = jnp.where(inside, 0.0, rows[r])
            if r in near:
                parts = [near[r][m] * spread[m] for m in range(8)]
                even = (parts[0] + parts[2]) + (parts[4] + parts[6])
                odd = (parts[1] + parts[3]) + (parts[5] + parts[7])
                rows[r] = kept - (even + odd)
            else:
                rows[r] = kept - change[8 * r : 8 * r + 8, :]
        rows[g] = panel
        if later:
            later.pop(0)()
    while later:
        later.pop(0)()
    return jnp.concatenate(rows, axis=0)


def solve_kernel(shift_ratio, scale, samples, gram_ref, target_ref, cent_hbm, out_ref, cent, sems):
    blocks = samples // 128
    chunks = sems.shape[0]
    wide = cent.shape[1] // chunks

    def load(m):
        at = pl.ds(m * wide, wide)
        return pltpu.make_async_copy(cent_hbm.at[:, at], cent.at[:, at], sems.at[m])

    for m in range(chunks):
        load(m).start()
    eye = lax.broadcasted_iota(jnp.int32, (128, 128), 0) == lax.broadcasted_iota(jnp.int32, (128, 128), 1)
    base = [0]
    for k in range(blocks):
        base.append(base[-1] + samples - 128 * k)
    trace = jnp.zeros((1, 1), F32)
    for k in range(blocks):
        trace += jnp.sum(jnp.where(eye, gram_ref[base[k] : base[k] + 128, :], 0.0), axis=(0, 1), keepdims=True)
    shift = shift_ratio * trace / samples
    shift = jnp.where(eye, jnp.broadcast_to(shift, (128, 128)), 0.0)
    rhs = []
    tiles, quot = {}, {}
    for k in range(blocks):
        for i in range(k, blocks):
            at = base[k] + 128 * (i - k)
            tiles[i, k] = gram_ref[at : at + 128, :] + shift if i == k else gram_ref[at : at + 128, :]
        rhs.append(jnp.broadcast_to(target_ref[0:1, 128 * k : 128 * k + 128], (8, 128)))

    def divide(i, k, inv):
        def run():
            quot[i, k] = dot_nn(tiles[i, k], inv)

        return run

    def reduce(i, j, k):
        def run():
            tiles[i, j] = tiles[i, j] - dot_nt(quot[i, k], tiles[j, k])

        return run

    def lower(i, k, right):
        def run():
            rhs[i] = rhs[i] - dot_nt(right, quot[i, k])

        return run

    def close(k, right, inv):
        def run():
            rhs[k] = dot_nn(right, inv)

        return run

    later = []
    for k in range(blocks):
        inv = -sweep_block(tiles[k, k], later)
        later = []
        if k < blocks - 1:
            divide(k + 1, k, inv)()
            reduce(k + 1, k + 1, k)()
            later += [divide(i, k, inv) for i in range(k + 2, blocks)]
            later += [reduce(i, k + 1, k) for i in range(k + 2, blocks)]
            later += [reduce(i, j, k) for j in range(k + 2, blocks) for i in range(j, blocks)]
            later += [lower(i, k, rhs[k]) for i in range(k + 1, blocks)]
        if k < blocks - 1:
            later.append(close(k, rhs[k], inv))
        else:
            close(k, rhs[k], inv)()
    found = [None] * blocks
    for k in reversed(range(blocks)):
        x = rhs[k]
        for i in range(k + 1, blocks):
            x = x - dot_nn(found[i], quot[i, k])
        found[k] = x
    coeffs = jnp.concatenate(found, axis=1).astype(BF16)
    for m in range(chunks):
        load(m).wait()
        part = jnp.dot(coeffs, cent[:, m * wide : (m + 1) * wide], preferred_element_type=F32) * scale
        for i in range(wide // 128):
            r = m * wide // 128 + i
            out_ref[r : r + 1, :] = part[0:1, 128 * i : 128 * (i + 1)]


def solve(gram, target, centered):
    samples, width = centered.shape
    blocks = samples // 128
    vmem = pl.BlockSpec(memory_space=pltpu.VMEM)
    return pl.pallas_call(
        functools.partial(solve_kernel, SHIFT_RATIO, -math.sqrt(D * FF), samples),
        out_shape=jax.ShapeDtypeStruct((width // 128, 128), F32),
        in_specs=[vmem, vmem, pl.BlockSpec(memory_space=pl.ANY)],
        out_specs=vmem,
        scratch_shapes=[
            pltpu.VMEM((samples, width), BF16),
            pltpu.SemaphoreType.DMA((8,)),
        ],
        compiler_params=pltpu.CompilerParams(vmem_limit_bytes=60 << 20),
        name="solve",
    )(gram, target, centered)


LSIDE = 10
GROUP = 4
WIDE = 8 * 65


def enter(ids):
    barrier = pltpu.get_barrier_semaphore()
    for device in ids:
        pl.semaphore_signal(barrier, inc=1, device_id=device, device_id_type=MESH)
    pl.semaphore_wait(barrier, len(ids))


def remote(src, dst, send, recv, device):
    copy = pltpu.make_async_remote_copy(
        src_ref=src, dst_ref=dst, send_sem=send, recv_sem=recv, device_id=device, device_id_type=MESH
    )
    copy.start()
    return copy


def describe(src, dst, send, recv, device):
    return pltpu.make_async_remote_copy(
        src_ref=src, dst_ref=dst, send_sem=send, recv_sem=recv, device_id=device, device_id_type=MESH
    )


def each(first, last, body):
    def step(k, carry):
        body(k)
        return carry

    lax.fori_loop(first, last, step, 0)


def make_target(spins_ref, offdiag_ref, norm_scale):
    signs = (2 * spins_ref[...] - 1).astype(F32)
    sites = signs.shape[0]
    column = lax.rem(lax.broadcasted_iota(jnp.int32, signs.shape, 0), LSIDE)

    def turn(values, by):
        return jnp.concatenate([values[by:], values[:by]], axis=0)

    def next_column(values):
        return jnp.where(column == LSIDE - 1, turn(values, sites - LSIDE + 1), turn(values, 1))

    def last_column(values):
        return jnp.where(column == 0, turn(values, LSIDE - 1), turn(values, sites - 1))

    down = turn(signs, LSIDE)
    near = jnp.sum(signs * (next_column(signs) + down), axis=0, keepdims=True)
    distant = jnp.sum(signs * (next_column(down) + last_column(down)), axis=0, keepdims=True)
    energies = 0.25 * (near + SECOND_RATIO * distant) + offdiag_ref[...]
    return (energies - jnp.mean(energies, axis=1, keepdims=True)) * norm_scale


def main_kernel(
    stream_hbm, win_ref, wout_ref, readout_ref, spins_ref, offdiag_ref, cent_out, gram_ref, target_ref, stream_ref,
    win, wout, hid, ht, hall, slope, acc, dsend, dl, dall, grad, cent, part_ref, twin, first, second,
    xs, xr, ws, wr, vs, vr, wws, wwr, vvs, vvr, sws, swr, svs, svr, hs, hr, ls, lr,
    sr, rr, sl, rl, fr, qr, fl, ql, bs, br, s0, r0, s1, r1, s2, r2, s3, r3, s4, r4, own, outs,
):
    s, p = lax.axis_index("samp"), lax.axis_index("par")
    x, c = s // 2, lax.rem(s, 2)
    y, z = p // 4, lax.rem(p, 4)
    sibling = s + 1 - 2 * c
    n = 16
    groups, tokens = 16, 25
    fetch = pltpu.make_async_copy(stream_hbm, stream_ref, own.at[3])
    fetch.start()
    rows, dims, width, samples = 112, 64, 128, 512
    norm_scale = 1.0 / math.sqrt(samples)
    right, left, far = lax.rem(s + 2, 8), lax.rem(s + 6, 8), lax.rem(s + 4, 8)
    pars = [lax.rem(p + k, 16) for k in range(1, 16)]
    lines = [(s, lax.rem(y + k, 4) * 4 + z) for k in range(1, 4)] + [(s, y * 4 + lax.rem(z + k, 4)) for k in range(1, 4)]
    enter(lines + [(lax.rem(s + k, 8), p) for k in range(1, 8)])

    def at(a, b):
        return lax.rem(y + a, 4) * 4 + lax.rem(z + b, 4)

    def origin(a, b):
        return at(4 - a, 4 - b)

    def xcopy(k):
        return describe(win_ref, win.at[p, x, c], xs.at[k - 1], xr.at[k - 1], (lax.rem(s + 2 * k, 8), p))

    def w_first(k):
        return describe(win.at[p, :, c], win.at[p, :, c], ws.at[k - 1], wr.at[k - 1], (s, at(k, 0)))

    def w_then(a, m):
        q, i = origin(a, 0), 3 * a + m - 1
        return describe(win.at[q, :, c], win.at[q, :, c], wws.at[i], wwr.at[i], (s, at(0, m)))

    def v_first(k):
        return describe(wout.at[p, c], wout.at[p, c], vs.at[k - 1], vr.at[k - 1], (s, at(0, k)))

    def v_then(b, m):
        q, i = origin(0, b), 3 * b + m - 1
        return describe(wout.at[q, c], wout.at[q, c], vvs.at[i], vvr.at[i], (s, at(m, 0)))

    def w_across(i):
        q = origin(i // 4, lax.rem(i, 4))
        return describe(win.at[q, :, c], win.at[q, :, c], sws.at[i], swr.at[i], (sibling, p))

    def v_across(i):
        q = origin(i // 4, lax.rem(i, 4))
        return describe(wout.at[q, c], wout.at[q, c], svs.at[i], svr.at[i], (sibling, p))

    def hcopy(k, c):
        to, at_c, i = lax.rem(s + k, 8), pl.ds(pl.multiple_of(4 * c, 4), 4), 4 * (k - 1) + c
        return describe(ht.at[to, at_c], hall.at[s, at_c], hs.at[i], hr.at[i], (to, p))

    def lcopy(k):
        q = lax.rem(p + k, n)
        return describe(dsend.at[q], dl.at[p], ls.at[k - 1], lr.at[k - 1], (s, q))

    mine_w = pltpu.make_async_copy(win_ref, win.at[p, x, c], own.at[0])
    mine_v = pltpu.make_async_copy(wout_ref.at[pl.ds(pl.multiple_of(64 * c, 64), 64)], wout.at[p, c], own.at[1])
    mine_w.start()
    mine_v.start()
    each(1, 4, lambda k: xcopy(k).start())
    mine_v.wait()
    each(1, 4, lambda k: v_first(k).start())
    each(1, 4, lambda m: v_then(0, m).start())
    v_across(0).start()
    mine_w.wait()

    def prepare(four):
        for v in range(2):
            pair = 2 * four + v
            values = stream_ref[:, pl.ds(pl.multiple_of(8 * pair, 8), 8), :]
            mean = jnp.mean(values, axis=-1, keepdims=True)
            centered = values - mean
            variance = jnp.mean(centered * centered, axis=-1, keepdims=True)
            scaled = centered * lax.rsqrt(variance + EPSILON)
            for half in range(2):
                u = 2 * v + half
                g = 4 * four + u
                pieces = [jnp.zeros((4 * u, 512), F32)] if u > 0 else []
                pieces += [scaled[t, 4 * half : 4 * half + 4] for t in range(tokens)]
                pieces += [jnp.zeros((width - 4 * tokens - 4 * u, 512), F32)]
                hidden = jnp.concatenate(pieces, axis=0)

                @pl.when(g == p)
                def _(hidden=hidden):
                    hid[...] = hidden[:rows].astype(BF16)

                flipped = jnp.transpose(hidden).astype(BF16)
                for q in range(8):
                    ht[q, g] = flipped[64 * q : 64 * (q + 1), :]

    def open_w():
        each(1, 4, lambda k: xcopy(k).wait_recv())
        each(1, 4, lambda k: w_first(k).start())
        each(1, 4, lambda m: w_then(0, m).start())
        w_across(0).start()

    def pass_v(k):
        v_first(k).wait_recv()
        each(1, 4, lambda m: v_then(k, m).start())
        v_across(k).start()

    def pass_w(k):
        w_first(k).wait_recv()
        each(1, 4, lambda m: w_then(k, m).start())
        w_across(4 * k).start()

    def work(step):
        @pl.when(step == 1)
        def _():
            each(1, 4, pass_v)

        @pl.when(step == 2)
        def _():
            each(1, 4, pass_w)

        prepare(step)
        each(1, 8, lambda k: hcopy(k, step).start())

        @pl.when(step == 0)
        def _():
            open_w()

    fetch.wait()
    each(0, 4, work)
    mine_h = pltpu.make_async_copy(ht.at[s], hall.at[s], own.at[2])
    mine_h.start()
    target_ref[...] = make_target(spins_ref, offdiag_ref, norm_scale)
    acc[...] = jnp.zeros_like(acc)

    def take(a):
        for b in range(4):
            if b > 0:
                w_then(a, b).wait_recv()
                w_across(4 * a + b).start()

            @pl.when(a > 0)
            def _():
                v_then(b, a).wait_recv()
                v_across(4 * a + b).start()

    def compute(a):
        row = lax.rem(y - a + 4, 4)
        for b in range(4):
            w_across(4 * a + b).wait_recv()
            v_across(4 * a + b).wait_recv()
        weights = jnp.concatenate([win[4 * row + j].reshape(512, 128) for j in range(4)], axis=1)
        preact = jnp.dot(hid[...], weights, preferred_element_type=F32)
        active, pull = jax.vjp(jax.nn.gelu, preact)
        slope[row] = pull(jnp.ones_like(preact))[0]
        acc[...] += jnp.dot(active.astype(BF16), wout[pl.ds(4 * row, 4)].reshape(512, 512), preferred_element_type=F32)

    take(0)

    def both(a):
        take(a)
        compute(a - 1)

    each(1, 4, both)
    compute(3)
    signal = (readout_ref[...] * jnp.tanh(acc[...])).astype(BF16)

    def back(i):
        row = lax.rem(y + jnp.where(i < 2, i, 5 - i), 4)
        weights = wout[pl.ds(4 * row, 4)].reshape(512, 512)
        backward = lax.dot_general(signal, weights, (((1,), (1,)), ((), ())), preferred_element_type=F32)
        delta = (backward * slope[row]).astype(BF16)
        for j in range(4):
            q = 4 * row + j
            dsend[q] = delta[:, 128 * j : 128 * (j + 1)]

            @pl.when(q != p)
            def _():
                lcopy(lax.rem(q - p + n, n)).start()

    each(0, 4, back)
    dl[p] = dsend[p]

    def chunk(i):
        return lax.rem(y + jnp.where(i == 0, 0, jnp.where(i == 1, 3, i - 1)), 4)

    def move(origin, i, send, recv, device):
        part = dall.at[origin, chunk(i)]
        return describe(part, part, send, recv, device)

    def to_right(i):
        return move(s, i, sr.at[i], rr.at[i], (right, p))

    def to_left(i):
        return move(s, i, sl.at[i], rl.at[i], (left, p))

    def on_right(j):
        return move(left, 2 * j, fr.at[j], qr.at[j], (right, p))

    def on_left(j):
        return move(right, 2 * j + 1, fl.at[j], ql.at[j], (left, p))

    def across(origin, i, slot):
        return move(origin, i, bs.at[slot + i], br.at[slot + i], (sibling, p))

    def begin(i):
        f = chunk(i)
        for j in range(4):
            q = 4 * f + j

            @pl.when(q != p)
            def _(q=q):
                lcopy(lax.rem(p - q + n, n)).wait_recv()

        for u in range(4):
            window = dl[4 * f + u]
            dall[s, f, 96 * u + 16 : 96 * u + 96, :] = window[16:96]
            if u == 0:
                dall[s, f, 0:16, :] = window[0:16]
            else:
                dall[s, f, 96 * u : 96 * u + 16, :] = window[0:16] + dl[4 * f + u - 1][96:112]
            if u == 3:
                dall[s, f, 384:400, :] = window[96:112]
        to_right(i).start()
        to_left(i).start()
        across(s, i, 0).start()

    each(0, 4, begin)
    mine_h.wait()

    lane = lax.broadcasted_iota(jnp.int32, (dims, width), 1)
    keep = [lax.rem(lane, GROUP) == i for i in range(GROUP)]
    fill = jnp.zeros((width - rows, 128), BF16)
    nothing = jnp.zeros((dims, width), BF16)

    def make(origin, i):
        f = chunk(i)
        for u in range(4):
            group = 4 * f + u
            flipped = hall[origin, group]
            delta = jnp.concatenate([dall[origin, f, 96 * u : 96 * u + rows, :], fill], axis=0)
            stack = jnp.concatenate([jnp.where(keep[v], flipped, nothing) for v in range(GROUP)], axis=0)
            grads = jnp.dot(stack, delta, preferred_element_type=F32).astype(BF16).astype(F32)
            for v in range(GROUP):
                grad[pl.ds(64 * origin + GROUP * group + v, dims, stride=WIDE), :] = grads[dims * v : dims * (v + 1), :]

    each(0, 4, lambda i: make(s, i))
    each(1, 8, lambda k: each(0, 4, lambda f: hcopy(k, f).wait_recv()))

    def near(i):
        to_right(i).wait_recv()
        to_left(i).wait_recv()

        @pl.when(lax.rem(i, 2) == 0)
        def _():
            on_right(i // 2).start()

        @pl.when(lax.rem(i, 2) == 1)
        def _():
            on_left(i // 2).start()

        across(left, i, 4).start()
        across(right, i, 8).start()
        make(left, i)
        make(right, i)

    each(0, 4, near)

    def beside(i):
        across(s, i, 0).wait_recv()
        make(sibling, i)

    each(0, 4, beside)

    def opposite(j):
        on_right(j).wait_recv()
        across(far, 2 * j, 12).start()
        on_left(j).wait_recv()
        across(far, 2 * j + 1, 12).start()
        make(far, 2 * j)
        make(far, 2 * j + 1)

    each(0, 2, opposite)

    def near_beside(i):
        across(left, i, 4).wait_recv()
        across(right, i, 8).wait_recv()
        make(sibling + left - s, i)
        make(sibling + right - s, i)

    each(0, 4, near_beside)

    def far_beside(i):
        across(far, i, 12).wait_recv()
        make(sibling + far - s, i)

    each(0, 4, far_beside)

    count = 4

    def center(m):
        for half in range(count):
            d = count * m + half
            values = grad[d * WIDE : d * WIDE + samples, :]
            mean = jnp.sum(values, axis=0, keepdims=True) * (1.0 / samples)
            cent[:, d * 128 : (d + 1) * 128] = ((values - mean) * norm_scale).astype(BF16)

    def store(m):
        at = pl.ds(m * 128 * count, 128 * count)
        return pltpu.make_async_copy(cent.at[:, at], cent_out.at[:, at], outs.at[m])

    def add(m):
        block = cent[:, m * 128 * count : (m + 1) * 128 * count]
        low = lax.dot_general(block, block[:256], (((1,), (1,)), ((), ())), preferred_element_type=F32)
        high = lax.dot_general(block[256:], block[256:], (((1,), (1,)), ((), ())), preferred_element_type=F32)
        for a, b, term in [(0, 512, low[:, :128]), (512, 896, low[128:, 128:]), (896, 1152, high[:, :128]), (1152, 1280, high[128:, 128:])]:
            if m == 0:
                part_ref[a:b, :] = term
            else:
                part_ref[a:b, :] += term

    steps = dims // count
    center(0)
    store(0).start()
    for m in range(1, steps):
        center(m)
        store(m).start()
        add(m - 1)
    add(steps - 1)

    core = c

    def slot(half, q):
        return pl.ds(pl.multiple_of(640 * half + 40 * q, 8), 40)

    give = pl.ds(pl.multiple_of(640 * (1 - core), 640), 640)
    keeps = pl.ds(pl.multiple_of(640 * core, 640), 640)
    copy = remote(part_ref.at[give], twin, s0.at[0], r0.at[0], (sibling, p))
    copy.wait_recv()
    part_ref[keeps, :] += twin[...]
    copies = [remote(part_ref.at[slot(core, q)], first.at[p], s1.at[k], r1.at[k], (s, q)) for k, q in enumerate(pars)]
    first[p] = part_ref[slot(core, p), :]
    for each_copy in copies:
        each_copy.wait_recv()
    total = first[0]
    for q in range(1, 16):
        total = total + first[q]
    second[x] = total
    more = [remote(second.at[x], second.at[x], s2.at[k], r2.at[k], (q, p)) for k, q in enumerate([right, far, left])]
    for each_copy in more:
        each_copy.wait_recv()
    total = second[0]
    for q in range(1, 4):
        total = total + second[q]
    gram_ref[slot(core, p), :] = total
    here = gram_ref.at[slot(core, p)]
    spread = [remote(here, here, s3.at[k], r3.at[k], (s, q)) for k, q in enumerate(pars)]
    passed = [remote(here, here, s4.at[15], r4.at[15], (sibling, p))]
    for k in range(15):
        spread[k].wait_recv()
        there = gram_ref.at[slot(core, lax.rem(p + 15 - k, 16))]
        passed.append(remote(there, there, s4.at[k], r4.at[k], (sibling, p)))
    for each_copy in passed:
        each_copy.wait()
    copy.wait_send()
    for each_copy in copies + more + spread:
        each_copy.wait_send()
    each(0, 4, lambda c: to_right(c).wait_send())
    each(0, 4, lambda c: to_left(c).wait_send())
    each(0, 2, lambda c: on_right(c).wait_send())
    each(0, 2, lambda c: on_left(c).wait_send())
    each(0, 4, lambda i: each(0, 4, lambda j: across(s, i, 4 * j).wait_send()))
    for m in range(steps):
        store(m).wait()
    each(1, n, lambda k: lcopy(k).wait_send())
    each(1, 8, lambda k: each(0, 4, lambda c: hcopy(k, c).wait_send()))
    each(1, 4, lambda k: xcopy(k).wait_send())
    each(1, 4, lambda k: w_first(k).wait_send())
    each(1, 4, lambda k: v_first(k).wait_send())
    each(0, 4, lambda k: each(1, 4, lambda m: w_then(k, m).wait_send()))
    each(0, 4, lambda k: each(1, 4, lambda m: v_then(k, m).wait_send()))
    each(0, n, lambda i: w_across(i).wait_send())
    each(0, n, lambda i: v_across(i).wait_send())


def make_gram(stream, weight_in, weight_out, readout, spins, offdiag):
    rows = 112
    sem = pltpu.SemaphoreType.DMA
    vmem = pl.BlockSpec(memory_space=pltpu.VMEM)
    counts = [3, 3, 3, 12, 12, 16, 16, 28, 15, 4, 4, 2, 2, 16, 1, 15, 3, 15, 16]
    return pl.pallas_call(
        main_kernel,
        out_shape=[
            jax.ShapeDtypeStruct((512, 8192), BF16),
            jax.ShapeDtypeStruct((1280, 128), F32),
            jax.ShapeDtypeStruct((1, 512), F32),
        ],
        in_specs=[pl.BlockSpec(memory_space=pl.ANY)] * 3 + [vmem] * 3,
        out_specs=[pl.BlockSpec(memory_space=pl.ANY), vmem, vmem],
        scratch_shapes=[
            pltpu.VMEM((25, 64, 512), F32),
            pltpu.VMEM((16, 4, 2, 64, 128), BF16),
            pltpu.VMEM((16, 2, 64, 512), BF16),
            pltpu.VMEM((rows, 512), BF16),
            pltpu.VMEM((8, 16, 64, 128), BF16),
            pltpu.VMEM((8, 16, 64, 128), BF16),
            pltpu.VMEM((4, rows, 512), F32),
            pltpu.VMEM((rows, 512), F32),
            pltpu.VMEM((16, rows, 128), BF16),
            pltpu.VMEM((16, rows, 128), BF16),
            pltpu.VMEM((8, 4, 400, 128), BF16),
            pltpu.VMEM((65 * WIDE, 128), F32),
            pltpu.VMEM((512, 8192), BF16),
            pltpu.VMEM((1280, 128), F32),
            pltpu.VMEM((640, 128), F32),
            pltpu.VMEM((16, 40, 128), F32),
            pltpu.VMEM((4, 40, 128), F32),
        ]
        + [sem((count,)) for count in counts for _ in range(2)]
        + [sem((4,)), sem((16,))],
        compiler_params=pltpu.CompilerParams(collective_id=1, has_side_effects=True, vmem_limit_bytes=60 << 20),
        name="make_gram",
    )(stream, weight_in, weight_out, readout, spins, offdiag)


def per_device(stream, weight_in, weight_out, readout, spins, offdiag):
    centered, gram, target = make_gram(
        jnp.transpose(stream, (1, 0, 2)), weight_in, weight_out, readout[None, :], jnp.transpose(spins), offdiag[None, :]
    )
    return solve(gram, target, centered)


def solution(mesh):
    return jax.shard_map(
        per_device,
        mesh=mesh,
        in_specs=(P("samp", None, None), P("samp", "par"), P("par", None), P(), P(), P()),
        out_specs=P("samp", "par"),
        check_vma=False,
    )
```
